32 devices in a mesh: group: 8 (over z, y), pencil: 4 (over x, core).
Axes of the slice: x: 2, y: 2, z: 4, core: 2. Of those that a mesh axis runs over, the one named last changes fastest.
Arguments:
- mult_iterate: float32 [8, 4, 8192], P('group', 'pencil'), may hold values from -6 to 6
- residual: float32 [8, 4, 8192], P('group', 'pencil'), may hold values from -6 to 6
- direction: float32 [8, 4, 8192], P('group', 'pencil'), may hold values from -6 to 6
- mult_scale: float32 [8, 4, 8192], P('group', 'pencil'), may hold values from 0.5 to 18
- eigen_basis: float32 [32, 3, 64, 64], P('group'), may hold values from -1 to 1
- eigen_values: float32 [32, 3, 64], P('group'), may hold values from 0.2 to 2
- elastic_coef: float32 [32, 3, 3], P('group'), may hold values from 0.5 to 2
- coarse_inverse: float32 [128, 128], replicated, may hold values from -1 to 2.5
- send_pos: int32 [8, 4, 16384], P('group', 'pencil'), may hold values from 0 to 48383, as said below
- pair_slots: int32 [8, 4, 2, 8192], P('group', 'pencil'), may hold values from 0 to 16383, as said below
- prim_rows: int32 [8, 4, 32], P('group', 'pencil'), may hold values from 0 to 16383, as said below
- coarse_idx: int32 [8, 4, 32], P('group', 'pencil'), may hold values from 0 to 127
Outputs:
- new_iterate: float32 [8, 4, 8192], P('group', 'pencil')
- new_residual: float32 [8, 4, 8192], P('group', 'pencil')
- new_direction: float32 [8, 4, 8192], P('group', 'pencil')
The draws below stay inside these ranges and needn't reach their ends.
Inputs may be any that keep to these rules, and one draw needn't show every extreme that they name: `send_pos`: distinct within each block (g, s). `pair_slots`: in each block (g, s) the two rows together hold every number of 0 to 16383 once. `prim_rows`: distinct within each block (g, s).
All inputs are finite; a program needn't handle non-finite values.
Results may differ from the reference program's by a relative error of at most 0.0003.
Values sent between devices are 32-bit elements; how exact they have to be, the bound alone decides.
A program may use at most 128 MiB of HBM per device.

```python
import math
import jax
import jax.numpy as jnp
from jax import lax

N = 64
C = 3
PG = 4
IFD = 16384
PRIM_DEV = 32
XS = 16
SHARE = 2048
MULT_DEV = 8192
NPAT = 32
NC = 128
N_GROUP = 8
N_PENCIL = 4


def draw_send_pos(key, part):
    face_count = XS * PG * C * (4 * N - 4)
    blocks = N_GROUP * N_PENCIL

    def one_block(block_key):
        interior = jax.random.permutation(block_key, face_count - 2).astype(jnp.int32) + 1
        chosen = jnp.concatenate([jnp.array([0, face_count - 1], jnp.int32), interior[:IFD - 2]])
        shuffle = jax.random.permutation(jax.random.fold_in(block_key, 7), IFD)
        return chosen[shuffle]
    picked = jax.vmap(one_block)(jax.random.split(key, blocks))
    return picked.reshape(N_GROUP, N_PENCIL, IFD).astype(jnp.int32)


def draw_pair_slots(key, part):
    blocks = N_GROUP * N_PENCIL

    def one_block(block_key):
        return jax.random.permutation(block_key, IFD).astype(jnp.int32).reshape(MULT_DEV, 2).T
    picked = jax.vmap(one_block)(jax.random.split(key, blocks))
    return picked.reshape(N_GROUP, N_PENCIL, 2, MULT_DEV)


def draw_prim_rows(key, part):
    blocks = N_GROUP * N_PENCIL

    def one_block(block_key):
        interior = jax.random.permutation(block_key, IFD - 2).astype(jnp.int32) + 1
        chosen = jnp.concatenate([jnp.array([0, IFD - 1], jnp.int32), interior[:PRIM_DEV - 2]])
        shuffle = jax.random.permutation(jax.random.fold_in(block_key, 11), PRIM_DEV)
        return chosen[shuffle]
    picked = jax.vmap(one_block)(jax.random.split(key, blocks))
    return picked.reshape(N_GROUP, N_PENCIL, PRIM_DEV)


def draw_mult_scale(key, part):
    shape = (N_GROUP, N_PENCIL, MULT_DEV)
    base_scale = jnp.exp(jax.random.uniform(key, shape, jnp.float32, math.log(0.5), math.log(2.0)))
    device = (jnp.arange(N_GROUP)[:, None] * N_PENCIL + jnp.arange(N_PENCIL)[None, :]).astype(jnp.float32)
    fraction = device / max(N_GROUP * N_PENCIL - 1, 1)
    growth = 3.0
    return base_scale * jnp.power(growth, fraction)[:, :, None]


def draw_eigen_basis(key, part):
    shape = (NPAT, 3, N, N)
    noise = jax.random.uniform(key, shape, jnp.float32, -1.0, 1.0)
    identity = jnp.eye(N, dtype=jnp.float32)
    return identity + noise * (0.5 / N) * (1.0 - identity)


def draw_coarse_inverse(key, part):
    noise = jax.random.uniform(key, (NC, NC), jnp.float32, -1.0, 1.0)
    mirror = 0.5 * (noise + noise.T)
    offdiag = jnp.cbrt(mirror) * (0.9 / NC)
    diagonal = jnp.exp(jax.random.uniform(jax.random.fold_in(key, 5), (NC,), jnp.float32, 0.0, math.log(2.5)))
    identity = jnp.eye(NC, dtype=jnp.float32)
    return offdiag * (1.0 - identity) + identity * diagonal[:, None]


def place_ends(drawn, own_key, low, high):
    shape = drawn.shape
    spot = [jax.random.randint(jax.random.fold_in(own_key, axis), (), 0, shape[axis]) for axis in range(len(shape))]
    drawn = drawn.at[tuple(spot)].set(low)
    longest = shape.index(max(shape))
    spot[longest] = (spot[longest] + 1) % shape[longest]
    return drawn.at[tuple(spot)].set(high)


def levels(stream_key, shape, shards, least, top_value):
    level = 1.0
    for dim, shards_of in shards:
        heights = jax.random.uniform(jax.random.fold_in(jax.random.fold_in(stream_key, 6), dim), (shards_of,), jnp.float32, least / len(shards), top_value / len(shards))
        level = level * jnp.repeat(jnp.exp(heights), shape[dim] // shards_of).reshape((-1,) + (1,) * (len(shape) - 1 - dim))
    return level


def bell_draw(stream_key, dims, width, limit, shards=(), kind=jnp.bfloat16):
    values = width * jax.random.normal(stream_key, dims, jnp.float32)
    if shards:
        values = values * levels(stream_key, dims, shards, -0.22, 0.18)
    return jnp.clip(values, -limit, limit).astype(kind)


def setup_inputs(seed: int = 0) -> dict:
    seeds = jax.random.split(jax.random.key(seed), 13)
    return {
        "mult_iterate": bell_draw(seeds[0], (N_GROUP, N_PENCIL, MULT_DEV), 1.0, 6.0, ((0, 8), (1, 4)), jnp.float32),
        "residual": bell_draw(seeds[1], (N_GROUP, N_PENCIL, MULT_DEV), 1.0, 6.0, ((0, 8), (1, 4)), jnp.float32),
        "direction": bell_draw(seeds[2], (N_GROUP, N_PENCIL, MULT_DEV), 1.0, 6.0, ((0, 8), (1, 4)), jnp.float32),
        "mult_scale": draw_mult_scale(jax.random.fold_in(seeds[12], 71), 0),
        "eigen_basis": draw_eigen_basis(jax.random.fold_in(seeds[12], 71), 0),
        "eigen_values": jnp.clip(jnp.exp(math.log(2.0) - 2.3025851 * jax.random.uniform(seeds[5], (NPAT, 3, N), jnp.float32) ** levels(seeds[5], (NPAT, 3, N), ((0, 8),), -0.2, 0.2)), 0.2, 2.0),
        "elastic_coef": jnp.clip(jnp.exp(math.log(2.0) - 1.3862944 * jax.random.uniform(seeds[6], (NPAT, C, 3), jnp.float32) ** levels(seeds[6], (NPAT, C, 3), ((0, 8),), -0.2, 0.2)), 0.5, 2.0),
        "coarse_inverse": draw_coarse_inverse(jax.random.fold_in(seeds[12], 71), 0),
        "send_pos": draw_send_pos(jax.random.fold_in(seeds[12], 71), 0),
        "pair_slots": draw_pair_slots(jax.random.fold_in(seeds[12], 71), 0),
        "prim_rows": draw_prim_rows(jax.random.fold_in(seeds[12], 71), 0),
        "coarse_idx": place_ends(jax.random.randint(seeds[11], (N_GROUP, N_PENCIL, PRIM_DEV), 0, NC), jax.random.fold_in(seeds[11], 1), 0, NC - 1).astype(jnp.int32),
    }


def face_to_flat(index, extent):
    cycle_size = 4 * extent - 4
    plane_index = index // cycle_size
    cycle_spot = index % cycle_size
    y_index = jnp.where(cycle_spot < extent, 0, jnp.where(cycle_spot < 2 * extent - 2, cycle_spot - extent + 1, jnp.where(cycle_spot < 3 * extent - 4, cycle_spot - (2 * extent - 2) + 1, extent - 1)))
    z_index = jnp.where(cycle_spot < extent, cycle_spot, jnp.where(cycle_spot < 2 * extent - 2, 0, jnp.where(cycle_spot < 3 * extent - 4, extent - 1, cycle_spot - (3 * extent - 4))))
    return (plane_index * extent * extent + y_index * extent + z_index).astype(jnp.int32)


def spectrum(coeffs, along_x, along_y, along_z):
    first = coeffs[None, :, :, 0, None, None] * along_x.T[:, :, None, None, None]
    second = coeffs[None, :, :, 1, None, None] * along_y[None, :, None, :, None]
    third = coeffs[None, :, :, 2, None, None] * along_z[None, :, None, None, :]
    return first + second + third


def transform_in(volume, basis):
    highest = lax.Precision.HIGHEST
    step_one = jnp.einsum('xpcyz,pzk->xpcyk', volume, basis[:, 2], precision=highest)
    step_two = jnp.einsum('xpcyk,pyj->xpcjk', step_one, basis[:, 1], precision=highest)
    return jnp.einsum('xpcjk,pxi->ipcjk', step_two, basis[:, 0], precision=highest)


def transform_out(volume, basis):
    highest = lax.Precision.HIGHEST
    step_one = jnp.einsum('ipcjk,pxi->xpcjk', volume, basis[:, 0], precision=highest)
    step_two = jnp.einsum('xpcjk,pyj->xpcyk', step_one, basis[:, 1], precision=highest)
    return jnp.einsum('xpcyk,pzk->xpcyz', step_two, basis[:, 2], precision=highest)


def place_slab(row_values, row_positions):
    slab_size = XS * PG * C * N * N
    return jnp.zeros((slab_size,), jnp.float32).at[row_positions].set(row_values)


def place_back(search_row, pair_row):
    return jnp.zeros((IFD,), jnp.float32).at[pair_row[0]].set(search_row).at[pair_row[1]].set(-search_row)


def add_primal(values_row, primal_row, coarse_row, lifted):
    return values_row.at[primal_row].add(lifted[coarse_row])


def group_solve(pieces):
    rows_group, positions_group, basis_group, values_group, coeffs_group = pieces
    slabs = jax.vmap(place_slab)(rows_group, positions_group)
    volume = slabs.reshape(N, PG, C, N, N)
    spectral = transform_in(volume, basis_group)
    scaled = spectral / spectrum(coeffs_group, values_group[:, 0], values_group[:, 1], values_group[:, 2])
    displace = transform_out(scaled, basis_group).reshape(N_PENCIL, XS * PG * C * N * N)
    return jnp.take_along_axis(displace, positions_group, axis=1)


def reference(mult_iterate, residual, direction, mult_scale, eigen_basis, eigen_values, elastic_coef, coarse_inverse, send_pos, pair_slots, prim_rows, coarse_idx):
    highest = lax.Precision.HIGHEST
    flat_pos = face_to_flat(send_pos, N)
    back = jax.vmap(jax.vmap(place_back))(direction, pair_slots)
    rows = back.reshape(N_GROUP, N_PENCIL, N_GROUP, SHARE).transpose(2, 1, 0, 3).reshape(N_GROUP, N_PENCIL, IFD)
    picked = lax.map(group_solve, (rows, flat_pos, eigen_basis.reshape(N_GROUP, PG, 3, N, N), eigen_values.reshape(N_GROUP, PG, 3, N), elastic_coef.reshape(N_GROUP, PG, C, 3)))
    primal_values = jnp.take_along_axis(picked, prim_rows, axis=2)
    coarse = jax.ops.segment_sum(primal_values.reshape(-1), coarse_idx.reshape(-1), num_segments=NC)
    lifted = jnp.dot(coarse_inverse, coarse, precision=highest)
    sent = jax.vmap(jax.vmap(add_primal, in_axes=(0, 0, 0, None)), in_axes=(0, 0, 0, None))(picked, prim_rows, coarse_idx, lifted)
    arrived = sent.reshape(N_GROUP, N_PENCIL, N_GROUP, SHARE).transpose(2, 1, 0, 3).reshape(N_GROUP, N_PENCIL, IFD)
    image = jnp.take_along_axis(arrived, pair_slots[:, :, 0], axis=2) - jnp.take_along_axis(arrived, pair_slots[:, :, 1], axis=2)
    old = jnp.sum(residual * mult_scale * residual)
    step_size = old / jnp.sum(direction * image)
    new_iterate = mult_iterate + step_size * direction
    new_residual = residual - step_size * image
    precond = mult_scale * new_residual
    new_norm = jnp.sum(new_residual * precond)
    new_direction = precond + (new_norm / old) * direction
    return (new_iterate, new_residual, new_direction)
```

```python
import functools

import jax
import jax.numpy as jnp
from jax import lax
from jax.experimental import pallas as pl
from jax.experimental.pallas import tpu as pltpu
from jax.sharding import PartitionSpec as P

LANES = 128
F32 = jnp.float32
BF16 = jnp.bfloat16
HIGHEST = lax.Precision.HIGHEST
MESH = pl.DeviceIdType.MESH
NT = (((1,), (1,)), ((), ()))
NN = (((1,), (0,)), ((), ()))


def exact_dot(left, right, dims=NN):
    return lax.dot_general(left, right, dims, precision=HIGHEST, preferred_element_type=F32)


def fast_dot(left, right, dims=NN):
    return lax.dot_general(left, right, dims, preferred_element_type=F32)


def halves(values):
    top = values.astype(BF16).astype(F32)
    return top, values - top


def floor_div(values, divisor):
    return ((values.astype(F32) + 0.5) * (1.0 / divisor)).astype(jnp.int32)


def iota(shape, dim):
    return lax.broadcasted_iota(jnp.int32, shape, dim)


def column(row):
    size = row.shape[1]
    diagonal = iota((size, size), 0) == iota((size, size), 1)
    return jnp.sum(jnp.where(diagonal, row, 0.0), axis=1, keepdims=True)


def one_hot(rows, count):
    return jnp.where(iota((count, rows.shape[1]), 0) == rows, 1.0, 0.0).astype(BF16)


def block_diagonal(blocks):
    total = sum(block.shape[1] for block in blocks)
    rows, before = [], 0
    for block in blocks:
        height, width = block.shape
        parts = [block]
        if before:
            parts = [jnp.zeros((height, before), F32)] + parts
        if total - before - width:
            parts = parts + [jnp.zeros((height, total - before - width), F32)]
        rows.append(jnp.concatenate(parts, axis=1) if len(parts) > 1 else block)
        before += width
    return jnp.concatenate(rows, axis=0)


def kernel(
    groups,
    pencils,
    iterate_ref,
    resid_ref,
    dir_ref,
    scale_ref,
    basis_ref,
    values_ref,
    coef_ref,
    inverse_ref,
    pos_ref,
    pair_ref,
    prim_ref,
    cidx_ref,
    iterate_out,
    resid_out,
    dir_out,
    back_acc,
    back_send,
    rows_in,
    row_of,
    slot_of,
    load_acc,
    load_send,
    load_in,
    diag_t,
    diag,
    diag_x,
    fwd,
    y_first,
    y_last,
    y_weight,
    bwd,
    out_send,
    out_in,
    table,
    picked,
    coarse_send,
    coarse_in,
    coarse_send2,
    coarse_in2,
    owner_in,
    image,
    sums_send,
    sums_in,
    sums_send2,
    sums_in2,
    a_send,
    a_recv,
    b_send,
    b_recv,
    c_send,
    c_recv,
    d_send,
    d_recv,
    d2_send,
    d2_recv,
    e_send,
    e_recv,
    f_send,
    f_recv,
    f2_send,
    f2_recv,
):
    group = lax.axis_index("group")
    pencil = lax.axis_index("pencil")
    patches, _, extent, _ = basis_ref.shape
    comps = coef_ref.shape[1]
    slab = extent // pencils
    share_rows = pos_ref.shape[1]
    row_blocks = groups * share_rows
    mult_rows = dir_ref.shape[0]
    slots = 4 * extent
    dup = pencils // patches
    local_i = extent // dup
    width = comps * local_i
    chunk = slab * comps
    table_rows = patches * chunk
    patch = pencil // dup
    part = lax.rem(pencil, dup)

    def group_peer(offset):
        return lax.rem(group + offset, groups)

    def pencil_peer(offset):
        return lax.rem(pencil + offset, pencils)

    def send_group(src_of, landing, send, recv):
        copies = []
        for offset in range(1, groups):
            peer = group_peer(offset)
            copy = pltpu.make_async_remote_copy(
                src_ref=src_of(peer),
                dst_ref=landing.at[group],
                send_sem=send.at[offset],
                recv_sem=recv.at[offset],
                device_id=(peer, pencil),
                device_id_type=MESH,
            )
            copy.start()
            copies.append(copy)
        return copies

    def send_pencil(src_of, landing, send, recv):
        copies = []
        for offset in range(1, pencils):
            peer = pencil_peer(offset)
            copy = pltpu.make_async_remote_copy(
                src_ref=src_of(peer),
                dst_ref=landing.at[pencil],
                send_sem=send.at[offset],
                recv_sem=recv.at[offset],
                device_id=(group, peer),
                device_id_type=MESH,
            )
            copy.start()
            copies.append(copy)
        return copies

    def finish(copies):
        for copy in copies:
            copy.wait_recv()
        for copy in copies:
            copy.wait_send()

    barrier = pltpu.get_barrier_semaphore()
    for offset in range(1, groups):
        pl.semaphore_signal(
            barrier, inc=1, device_id=(group_peer(offset), pencil), device_id_type=MESH
        )
    for offset in range(1, pencils):
        pl.semaphore_signal(
            barrier, inc=1, device_id=(group, pencil_peer(offset)), device_id_type=MESH
        )

    back_acc[...] = jnp.zeros_like(back_acc)

    def back_step(block, carry):
        base = pl.multiple_of(block * 8, 8)
        lane_base = pl.multiple_of(block * 8 * LANES, 8 * LANES)
        values = dir_ref[pl.ds(base, 8), :]
        pairs = pair_ref[:, pl.ds(lane_base, 8 * LANES)]
        high = lax.shift_right_logical(pairs, 7)
        low = jnp.bitwise_and(pairs, LANES - 1)
        tops, rests = halves(values)
        left, right = [], []
        for i in range(8):
            lanes = slice(i * LANES, (i + 1) * LANES)
            for side, sign in ((0, 1.0), (1, -1.0)):
                here = iota((row_blocks, LANES), 0) == high[side : side + 1, lanes]
                left.append(
                    jnp.concatenate(
                        [
                            jnp.where(here, sign * tops[i : i + 1], 0.0).astype(BF16),
                            jnp.where(here, sign * rests[i : i + 1], 0.0).astype(BF16),
                        ],
                        axis=0,
                    )
                )
                right.append(one_hot(low[side : side + 1, lanes], LANES))
        back_acc[...] += fast_dot(
            jnp.concatenate(left, axis=1), jnp.concatenate(right, axis=1), NT
        )
        return carry

    lax.fori_loop(0, mult_rows // 8, back_step, 0)
    for h in range(groups):
        rows = slice(h * share_rows, (h + 1) * share_rows)
        low_rows = slice(row_blocks + h * share_rows, row_blocks + (h + 1) * share_rows)
        back_send[h] = back_acc[rows, :] + back_acc[low_rows, :]

    pl.semaphore_wait(barrier, groups + pencils - 2)
    copies_a = send_group(lambda peer: back_send.at[peer], rows_in, a_send, a_recv)
    rows_in[group] = back_send[group]

    cells = pos_ref[...]
    cycle = 4 * extent - 4
    plane = floor_div(cells, cycle)
    spot = cells - plane * cycle
    slot_of[...] = (
        spot
        + jnp.where(spot >= extent, 1, 0)
        + jnp.where(spot >= 2 * extent - 2, 2, 0)
        + jnp.where(spot >= 3 * extent - 4, 1, 0)
    )
    x_index = floor_div(plane, patches * comps)
    rest = plane - x_index * (patches * comps)
    p_index = floor_div(rest, comps)
    c_index = rest - p_index * comps
    row_of[...] = p_index * chunk + c_index * slab + x_index

    basis_x = basis_ref[patch, 0]
    basis_y = basis_ref[patch, 1]
    basis_z = basis_ref[patch, 2]
    spectrum = values_ref[patch]
    along_x = spectrum[0:1]
    if dup > 1:
        basis_x = sum(
            jnp.where(part == u, basis_x[:, u * local_i : (u + 1) * local_i], 0.0)
            for u in range(dup)
        )
        along_x = sum(
            jnp.where(part == u, along_x[:, u * local_i : (u + 1) * local_i], 0.0)
            for u in range(dup)
        )
    diag[...] = block_diagonal([basis_z, basis_y, basis_y, basis_z])
    basis_yt, basis_zt = basis_y.T, basis_z.T
    diag_t[...] = block_diagonal([basis_zt, basis_yt, basis_yt, basis_zt])
    diag_x[...] = block_diagonal([basis_x] * comps)
    coef = coef_ref[patch]
    ones = jnp.ones((1, local_i), F32)
    weight_x = jnp.concatenate([coef[c : c + 1, 0:1] * along_x for c in range(comps)], axis=1)
    weight_y = jnp.concatenate([coef[c : c + 1, 1:2] * ones for c in range(comps)], axis=1)
    weight_z = jnp.concatenate([coef[c : c + 1, 2:3] * ones for c in range(comps)], axis=1)
    y_weight[...] = column(spectrum[1:2]) * weight_y
    wide = jnp.ones((1, width), F32)
    y_first[...] = column(basis_y[0:1]) * wide
    y_last[...] = column(basis_y[extent - 1 : extent]) * wide
    xz_weight = weight_x + column(spectrum[2:3]) * weight_z
    z_first = column(basis_z[0:1]) * wide
    z_last = column(basis_z[extent - 1 : extent]) * wide
    load_acc[...] = jnp.zeros_like(load_acc)
    finish(copies_a)

    def load_step(h, carry):
        values = rows_in[h]
        rows, columns = row_of[h], slot_of[h]
        tops, rests = halves(values)
        left, right = [], []
        for i in range(share_rows):
            here = iota((table_rows, LANES), 0) == rows[i : i + 1]
            left.append(
                jnp.concatenate(
                    [
                        jnp.where(here, tops[i : i + 1], 0.0).astype(BF16),
                        jnp.where(here, rests[i : i + 1], 0.0).astype(BF16),
                    ],
                    axis=0,
                )
            )
            right.append(one_hot(columns[i : i + 1], slots))
        load_acc[...] += fast_dot(
            jnp.concatenate(left, axis=1), jnp.concatenate(right, axis=1), NT
        )
        return carry

    lax.fori_loop(0, groups, load_step, 0)
    for p in range(patches):
        load_send[p] = (
            load_acc[p * chunk : (p + 1) * chunk, :]
            + load_acc[table_rows + p * chunk : table_rows + (p + 1) * chunk, :]
        )
    copies_b = send_pencil(lambda peer: load_send.at[peer // dup], load_in, b_send, b_recv)
    load_in[pencil] = load_send[patch]
    finish(copies_b)

    sides = jnp.concatenate(
        [load_in[s, c * slab : (c + 1) * slab, :] for c in range(comps) for s in range(pencils)],
        axis=0,
    )
    fwd[...] = exact_dot(exact_dot(diag_t[...], sides, NT), diag_x[...])
    side_a = fwd[0:extent, :]
    side_d = fwd[3 * extent : 4 * extent, :]

    def solve_step(block, carry):
        sum_first, sum_last = carry
        base = pl.multiple_of(block * 8, 8)
        first = y_first[pl.ds(base, 8), :]
        last = y_last[pl.ds(base, 8), :]
        weight = y_weight[pl.ds(base, 8), :]
        side_b = fwd[pl.ds(extent + base, 8), :]
        side_c = fwd[pl.ds(2 * extent + base, 8), :]
        out_b, out_c = [], []
        for i in range(8):
            row = slice(i, i + 1)
            spectral = (
                first[row] * side_a + last[row] * side_d + side_b[row] * z_first + side_c[row] * z_last
            )
            scaled = spectral / (xz_weight + weight[row])
            sum_first = sum_first + first[row] * scaled
            sum_last = sum_last + last[row] * scaled
            out_b.append(jnp.sum(z_first * scaled, axis=0, keepdims=True))
            out_c.append(jnp.sum(z_last * scaled, axis=0, keepdims=True))
        bwd[pl.ds(extent + base, 8), :] = jnp.concatenate(out_b, axis=0)
        bwd[pl.ds(2 * extent + base, 8), :] = jnp.concatenate(out_c, axis=0)
        return sum_first, sum_last

    zero = jnp.zeros((extent, width), F32)
    sum_first, sum_last = lax.fori_loop(0, extent // 8, solve_step, (zero, zero))
    bwd[0:extent, :] = sum_first
    bwd[3 * extent : 4 * extent, :] = sum_last
    cells_out = exact_dot(diag_x[...], exact_dot(diag[...], bwd[...]), NT)
    for s in range(pencils):
        out_send[s] = jnp.concatenate(
            [
                cells_out[c * extent + s * slab : c * extent + (s + 1) * slab, :]
                for c in range(comps)
            ],
            axis=0,
        )
    copies_c = send_pencil(lambda peer: out_send.at[peer], out_in, c_send, c_recv)
    out_in[pencil] = out_send[pencil]
    finish(copies_c)

    for p in range(patches):
        total = out_in[p * dup]
        for u in range(1, dup):
            total = total + out_in[p * dup + u]
        top, rest_part = halves(total)
        table[p * chunk : (p + 1) * chunk, :] = top
        table[table_rows + p * chunk : table_rows + (p + 1) * chunk, :] = rest_part
    lookup = table[...].astype(BF16)

    def pick_step(h, carry):
        rows, columns = row_of[h], slot_of[h]
        found = []
        for i in range(0, share_rows, 2):
            hot = jnp.concatenate(
                [one_hot(columns[i : i + 1], slots), one_hot(columns[i + 1 : i + 2], slots)], axis=1
            )
            both = fast_dot(lookup, hot)
            both = both[0:table_rows] + both[table_rows : 2 * table_rows]
            for u in range(2):
                here = iota((table_rows, LANES), 0) == rows[i + u : i + u + 1]
                found.append(
                    jnp.sum(
                        jnp.where(here, both[:, u * LANES : (u + 1) * LANES], 0.0),
                        axis=0,
                        keepdims=True,
                    )
                )
        picked[h] = jnp.concatenate(found, axis=0)
        return carry

    lax.fori_loop(0, groups, pick_step, 0)

    primal = prim_ref[...]
    count = primal.shape[1]
    prim_high = lax.shift_right_logical(primal, 7)
    prim_low = jnp.bitwise_and(primal, LANES - 1)
    hot_high = jnp.where(iota((row_blocks, count), 0) == prim_high, 1.0, 0.0)
    hot_low = jnp.where(iota((LANES, count), 0) == prim_low, 1.0, 0.0)
    coarse_count = inverse_ref.shape[0]
    hot_coarse = jnp.where(iota((coarse_count, count), 0) == cidx_ref[...], 1.0, 0.0)
    flat = jnp.concatenate([picked[h] for h in range(groups)], axis=0)
    primal_values = jnp.sum(exact_dot(flat, hot_low) * hot_high, axis=0, keepdims=True)
    coarse_send[...] = exact_dot(jnp.broadcast_to(primal_values, (8, count)), hot_coarse, NT)
    copies_d = send_pencil(lambda peer: coarse_send, coarse_in, d_send, d_recv)
    coarse_in[pencil] = coarse_send[...]
    finish(copies_d)
    coarse_send2[...] = sum(coarse_in[s] for s in range(pencils))
    copies_d2 = send_group(lambda peer: coarse_send2, coarse_in2, d2_send, d2_recv)
    coarse_in2[group] = coarse_send2[...]
    finish(copies_d2)
    coarse = sum(coarse_in2[h] for h in range(groups))
    lifted = exact_dot(coarse, inverse_ref[...], NT)
    added = exact_dot(lifted, hot_coarse)[0:1]
    added_rows = exact_dot(hot_high * added, hot_low, NT)
    for h in range(groups):
        picked[h] = picked[h] + added_rows[h * share_rows : (h + 1) * share_rows, :]
    copies_e = send_group(lambda peer: picked.at[peer], owner_in, e_send, e_recv)
    owner_in[group] = picked[group]
    finish(copies_e)

    owners = jnp.concatenate([owner_in[h] for h in range(groups)], axis=0)
    top, rest_part = halves(owners)
    owner_table = jnp.concatenate([top, rest_part], axis=1).astype(BF16)

    def image_step(block, carry):
        base = pl.multiple_of(block * 8, 8)
        lane_base = pl.multiple_of(block * 8 * LANES, 8 * LANES)
        pairs = pair_ref[:, pl.ds(lane_base, 8 * LANES)]
        high = lax.shift_right_logical(pairs, 7)
        low = jnp.bitwise_and(pairs, LANES - 1)
        found = []
        for i in range(8):
            lanes = slice(i * LANES, (i + 1) * LANES)
            hot = jnp.concatenate(
                [one_hot(low[0:1, lanes], LANES), one_hot(low[1:2, lanes], LANES)], axis=1
            )
            both = fast_dot(owner_table, jnp.concatenate([hot, hot], axis=0))
            place = iota((row_blocks, LANES), 0)
            jump = jnp.where(place == high[0:1, lanes], both[:, 0:LANES], 0.0) - jnp.where(
                place == high[1:2, lanes], both[:, LANES : 2 * LANES], 0.0
            )
            found.append(jnp.sum(jump, axis=0, keepdims=True))
        image[pl.ds(base, 8), :] = jnp.concatenate(found, axis=0)
        return carry

    lax.fori_loop(0, mult_rows // 8, image_step, 0)

    resid, search, scale, jumps = resid_ref[...], dir_ref[...], scale_ref[...], image[...]
    scaled_resid, scaled_jump = scale * resid, scale * jumps

    def lane_sums(values):
        return jnp.sum(values, axis=0, keepdims=True)

    sums_send[...] = jnp.concatenate(
        [
            lane_sums(resid * scaled_resid),
            lane_sums(search * jumps),
            lane_sums(scaled_resid * jumps),
            lane_sums(scaled_jump * jumps),
            jnp.zeros((4, LANES), F32),
        ],
        axis=0,
    )
    copies_f = send_pencil(lambda peer: sums_send, sums_in, f_send, f_recv)
    sums_in[pencil] = sums_send[...]
    finish(copies_f)
    sums_send2[...] = sum(sums_in[s] for s in range(pencils))
    copies_f2 = send_group(lambda peer: sums_send2, sums_in2, f2_send, f2_recv)
    sums_in2[group] = sums_send2[...]
    finish(copies_f2)
    totals = jnp.sum(sum(sums_in2[h] for h in range(groups)), axis=1, keepdims=True)
    old, curvature = totals[0:1], totals[1:2]
    alpha = old / curvature
    new = old - 2.0 * alpha * totals[2:3] + alpha * (alpha * totals[3:4])
    next_resid = resid - alpha * jumps
    iterate_out[...] = iterate_ref[...] + alpha * search
    resid_out[...] = next_resid
    dir_out[...] = scale * next_resid + (new / old) * search


def body(
    groups,
    pencils,
    mult_iterate,
    residual,
    direction,
    mult_scale,
    eigen_basis,
    eigen_values,
    elastic_coef,
    coarse_inverse,
    send_pos,
    pair_slots,
    prim_rows,
    coarse_idx,
):
    mult_count = direction.shape[-1]
    mult_rows = mult_count // LANES
    rows_count = send_pos.shape[-1]
    row_blocks = rows_count // LANES
    share_rows = row_blocks // groups
    patches, _, extent, _ = eigen_basis.shape
    comps = elastic_coef.shape[1]
    slab = extent // pencils
    slots = 4 * extent
    width = comps * extent // (pencils // patches)
    chunk = slab * comps
    table_rows = patches * chunk
    coarse_count = coarse_inverse.shape[0]

    def vmem(*shape):
        return pltpu.VMEM(shape, F32)

    def index(*shape):
        return pltpu.VMEM(shape, jnp.int32)

    share = (groups, share_rows, LANES)
    pencil_sems = pltpu.SemaphoreType.DMA((pencils,))
    group_sems = pltpu.SemaphoreType.DMA((groups,))
    scratch = [
        vmem(2 * row_blocks, LANES),
        vmem(*share),
        vmem(*share),
        index(*share),
        index(*share),
        vmem(2 * table_rows, slots),
        vmem(patches, chunk, slots),
        vmem(pencils, chunk, slots),
        vmem(slots, slots),
        vmem(slots, slots),
        vmem(comps * extent, width),
        vmem(slots, width),
        vmem(extent, width),
        vmem(extent, width),
        vmem(extent, width),
        vmem(slots, width),
        vmem(pencils, chunk, slots),
        vmem(pencils, chunk, slots),
        vmem(2 * table_rows, slots),
        vmem(*share),
        vmem(8, coarse_count),
        vmem(pencils, 8, coarse_count),
        vmem(8, coarse_count),
        vmem(groups, 8, coarse_count),
        vmem(*share),
        vmem(mult_rows, LANES),
        vmem(8, LANES),
        vmem(pencils, 8, LANES),
        vmem(8, LANES),
        vmem(groups, 8, LANES),
        group_sems,
        group_sems,
        pencil_sems,
        pencil_sems,
        pencil_sems,
        pencil_sems,
        pencil_sems,
        pencil_sems,
        group_sems,
        group_sems,
        group_sems,
        group_sems,
        pencil_sems,
        pencil_sems,
        group_sems,
        group_sems,
    ]
    shape = (mult_rows, LANES)
    outs = pl.pallas_call(
        functools.partial(kernel, groups, pencils),
        out_shape=[jax.ShapeDtypeStruct(shape, F32)] * 3,
        in_specs=[pl.BlockSpec(memory_space=pltpu.VMEM)] * 12,
        out_specs=[pl.BlockSpec(memory_space=pltpu.VMEM)] * 3,
        scratch_shapes=scratch,
        compiler_params=pltpu.CompilerParams(
            collective_id=0, has_side_effects=True, vmem_limit_bytes=48 * 1024 * 1024
        ),
        name="tearing_step",
    )(
        mult_iterate.reshape(shape),
        residual.reshape(shape),
        direction.reshape(shape),
        mult_scale.reshape(shape),
        eigen_basis,
        eigen_values,
        elastic_coef,
        coarse_inverse,
        send_pos.reshape(share),
        pair_slots.reshape(pair_slots.shape[2:]),
        prim_rows.reshape(1, -1),
        coarse_idx.reshape(1, -1),
    )
    return tuple(out.reshape(1, 1, mult_count) for out in outs)


def solution(mesh):
    rows = P("group", "pencil", None)
    in_specs = (
        rows,
        rows,
        rows,
        rows,
        P("group", None, None, None),
        P("group", None, None),
        P("group", None, None),
        P(),
        rows,
        P("group", "pencil", None, None),
        rows,
        rows,
    )
    return jax.shard_map(
        functools.partial(body, mesh.shape["group"], mesh.shape["pencil"]),
        mesh=mesh,
        in_specs=in_specs,
        out_specs=(rows, rows, rows),
        check_vma=False,
    )
```

```python
import functools

import jax
import jax.numpy as jnp
from jax import lax
from jax.experimental import pallas as pl
from jax.experimental.pallas import tpu as pltpu
from jax.sharding import PartitionSpec as P

LANES = 128
F32 = jnp.float32
BF16 = jnp.bfloat16
HIGHEST = lax.Precision.HIGHEST
MESH = pl.DeviceIdType.MESH
NT = (((1,), (1,)), ((), ()))
NN = (((1,), (0,)), ((), ()))


def exact_dot(left, right, dims=NN):
    return lax.dot_general(left, right, dims, precision=HIGHEST, preferred_element_type=F32)


def fast_dot(left, right, dims=NN):
    return lax.dot_general(left, right, dims, preferred_element_type=F32)


def halves(values):
    top = values.astype(BF16).astype(F32)
    return top, values - top


def floor_div(values, divisor):
    return ((values.astype(F32) + 0.5) * (1.0 / divisor)).astype(jnp.int32)


def iota(shape, dim):
    return lax.broadcasted_iota(jnp.int32, shape, dim)


def column(row):
    size = row.shape[1]
    diagonal = iota((size, size), 0) == iota((size, size), 1)
    return jnp.sum(jnp.where(diagonal, row, 0.0), axis=1, keepdims=True)


def numbers(count):
    return iota((count, LANES), 0).astype(F32).astype(BF16).reshape(count // 16, 16, LANES)


def packed(row):
    return jnp.broadcast_to(row, (16, LANES)).astype(BF16)[None]


def placed(counts, row, *values):
    here = counts == packed(row)
    size = counts.shape[0] * 16
    zero = jnp.zeros((), BF16)
    return [jnp.where(here, packed(value), zero).reshape(size, LANES) for value in values]


def one_hot(counts, row):
    here = counts == packed(row)
    return jnp.where(here, jnp.ones((), BF16), jnp.zeros((), BF16)).reshape(-1, LANES)


def block_diagonal(blocks):
    total = sum(block.shape[1] for block in blocks)
    rows, before = [], 0
    for block in blocks:
        height, width = block.shape
        parts = [block]
        if before:
            parts = [jnp.zeros((height, before), F32)] + parts
        if total - before - width:
            parts = parts + [jnp.zeros((height, total - before - width), F32)]
        rows.append(jnp.concatenate(parts, axis=1) if len(parts) > 1 else block)
        before += width
    return jnp.concatenate(rows, axis=0)


def kernel(
    groups,
    pencils,
    resid_hbm,
    dir_hbm,
    scale_hbm,
    basis_hbm,
    values_hbm,
    coef_hbm,
    inverse_hbm,
    pos_hbm,
    pair_hbm,
    prim_hbm,
    cidx_hbm,
    image_out,
    alpha_out,
    beta_out,
    back_acc,
    back_send,
    rows_in,
    row_of,
    slot_of,
    load_acc,
    load_send,
    load_in,
    diag_t,
    diag,
    diag_x,
    fwd,
    y_first,
    y_last,
    y_weight,
    bwd,
    out_send,
    out_in,
    table,
    picked,
    coarse_send,
    coarse_in,
    coarse_send2,
    coarse_in2,
    owner_in,
    image,
    sums_send,
    sums_in,
    sums_send2,
    sums_in2,
    a_send,
    a_recv,
    b_send,
    b_recv,
    c_send,
    c_recv,
    d_send,
    d_recv,
    d2_send,
    d2_recv,
    e_send,
    e_recv,
    f_send,
    f_recv,
    f2_send,
    f2_recv,
    resid_ref,
    dir_ref,
    scale_ref,
    basis_ref,
    values_ref,
    coef_ref,
    inverse_ref,
    pos_ref,
    pair_ref,
    prim_ref,
    cidx_ref,
    xz_weight,
    z_first,
    z_last,
    input_sem,
):
    group = lax.axis_index("group")
    pencil = lax.axis_index("pencil")
    patches, _, extent, _ = basis_hbm.shape
    comps = coef_hbm.shape[0]
    slab = extent // pencils
    share_rows = pos_ref.shape[1]
    row_blocks = groups * share_rows
    mult_rows = dir_ref.shape[0]
    slots = 4 * extent
    dup = pencils // patches
    local_i = extent // dup
    width = comps * local_i
    chunk = slab * comps
    table_rows = patches * chunk
    patch = pencil // dup
    part = lax.rem(pencil, dup)

    def group_peer(offset):
        return lax.rem(group + offset, groups)

    def pencil_peer(offset):
        return lax.rem(pencil + offset, pencils)

    def send_group(src_of, landing, send, recv):
        copies = []
        for offset in range(1, groups):
            peer = group_peer(offset)
            copy = pltpu.make_async_remote_copy(
                src_ref=src_of(peer),
                dst_ref=landing.at[group],
                send_sem=send.at[offset],
                recv_sem=recv.at[offset],
                device_id=(peer, pencil),
                device_id_type=MESH,
            )
            copy.start()
            copies.append(copy)
        return copies

    def send_pencil(src_of, landing, send, recv):
        copies = []
        for offset in range(1, pencils):
            peer = pencil_peer(offset)
            copy = pltpu.make_async_remote_copy(
                src_ref=src_of(peer),
                dst_ref=landing.at[pencil],
                send_sem=send.at[offset],
                recv_sem=recv.at[offset],
                device_id=(group, peer),
                device_id_type=MESH,
            )
            copy.start()
            copies.append(copy)
        return copies

    def finish(copies):
        for copy in copies:
            copy.wait_recv()
        for copy in copies:
            copy.wait_send()

    barrier = pltpu.get_barrier_semaphore()
    for offset in range(1, groups):
        pl.semaphore_signal(
            barrier, inc=1, device_id=(group_peer(offset), pencil), device_id_type=MESH
        )
    for offset in range(1, pencils):
        pl.semaphore_signal(
            barrier, inc=1, device_id=(group, pencil_peer(offset)), device_id_type=MESH
        )

    inputs = {}
    for number, (name, source, target) in enumerate(
        [
            ("dir", dir_hbm, dir_ref),
            ("pair", pair_hbm, pair_ref),
            ("pos", pos_hbm, pos_ref),
            ("basis", basis_hbm.at[patch], basis_ref),
            ("values", values_hbm, values_ref),
            ("coef", coef_hbm, coef_ref),
            ("prim", prim_hbm, prim_ref),
            ("cidx", cidx_hbm, cidx_ref),
            ("inverse", inverse_hbm, inverse_ref),
            ("resid", resid_hbm, resid_ref),
            ("scale", scale_hbm, scale_ref),
        ]
    ):
        inputs[name] = pltpu.make_async_copy(source, target, input_sem.at[number])
        inputs[name].start()

    back_acc[...] = jnp.zeros_like(back_acc)
    row_numbers = numbers(row_blocks)
    lane_numbers = numbers(LANES)
    slot_numbers = numbers(slots)
    table_numbers = numbers(table_rows)
    inputs["dir"].wait()
    inputs["pair"].wait()

    def back_step(block, carry):
        base = pl.multiple_of(block * 8, 8)
        lane_base = pl.multiple_of(block * 8 * LANES, 8 * LANES)
        values = dir_ref[pl.ds(base, 8), :]
        pairs = pair_ref[:, pl.ds(lane_base, 8 * LANES)]
        high = lax.shift_right_logical(pairs, 7).astype(F32)
        low = jnp.bitwise_and(pairs, LANES - 1).astype(F32)
        tops, rests = halves(values)
        left, right = [], []
        for i in range(8):
            lanes = slice(i * LANES, (i + 1) * LANES)
            for side, sign in ((0, 1.0), (1, -1.0)):
                left.append(
                    jnp.concatenate(
                        placed(
                            row_numbers,
                            high[side : side + 1, lanes],
                            sign * tops[i : i + 1],
                            sign * rests[i : i + 1],
                        ),
                        axis=0,
                    )
                )
                right.append(one_hot(lane_numbers, low[side : side + 1, lanes]))
        back_acc[...] += fast_dot(
            jnp.concatenate(left, axis=1), jnp.concatenate(right, axis=1), NT
        )
        return carry

    lax.fori_loop(0, mult_rows // 8, back_step, 0)
    for h in range(groups):
        rows = slice(h * share_rows, (h + 1) * share_rows)
        low_rows = slice(row_blocks + h * share_rows, row_blocks + (h + 1) * share_rows)
        back_send[h] = back_acc[rows, :] + back_acc[low_rows, :]

    pl.semaphore_wait(barrier, groups + pencils - 2)
    copies_a = send_group(lambda peer: back_send.at[peer], rows_in, a_send, a_recv)
    rows_in[group] = back_send[group]

    for name in ("pos", "basis", "values", "coef"):
        inputs[name].wait()
    cells = pos_ref[...]
    cycle = 4 * extent - 4
    plane = floor_div(cells, cycle)
    spot = cells - plane * cycle
    slot_of[...] = (
        spot
        + jnp.where(spot >= extent, 1, 0)
        + jnp.where(spot >= 2 * extent - 2, 2, 0)
        + jnp.where(spot >= 3 * extent - 4, 1, 0)
    ).astype(F32)
    x_index = floor_div(plane, patches * comps)
    rest = plane - x_index * (patches * comps)
    p_index = floor_div(rest, comps)
    c_index = rest - p_index * comps
    row_of[...] = (p_index * chunk + c_index * slab + x_index).astype(F32)

    basis_x = basis_ref[0]
    basis_y = basis_ref[1]
    basis_z = basis_ref[2]

    def of_patch(ref, row):
        return sum(jnp.where(patch == p, ref[row, p : p + 1, :], 0.0) for p in range(patches))

    spectrum = [of_patch(values_ref, axis) for axis in range(3)]
    coef = [of_patch(coef_ref, c) for c in range(comps)]
    along_x = spectrum[0]
    if dup > 1:
        basis_x = sum(
            jnp.where(part == u, basis_x[:, u * local_i : (u + 1) * local_i], 0.0)
            for u in range(dup)
        )
        along_x = sum(
            jnp.where(part == u, along_x[:, u * local_i : (u + 1) * local_i], 0.0)
            for u in range(dup)
        )
    diag[...] = block_diagonal([basis_z, basis_y, basis_y, basis_z])
    basis_yt, basis_zt = basis_y.T, basis_z.T
    diag_t[...] = block_diagonal([basis_zt, basis_yt, basis_yt, basis_zt])
    diag_x[...] = block_diagonal([basis_x] * comps)
    ones = jnp.ones((1, local_i), F32)
    weight_x = jnp.concatenate([coef[c][:, 0:1] * along_x for c in range(comps)], axis=1)
    weight_y = jnp.concatenate([coef[c][:, 1:2] * ones for c in range(comps)], axis=1)
    weight_z = jnp.concatenate([coef[c][:, 2:3] * ones for c in range(comps)], axis=1)
    y_weight[...] = column(spectrum[1]) * weight_y
    wide = jnp.ones((1, width), F32)
    y_first[...] = column(basis_y[0:1]) * wide
    y_last[...] = column(basis_y[extent - 1 : extent]) * wide
    xz_weight[...] = weight_x + column(spectrum[2]) * weight_z
    z_first[...] = column(basis_z[0:1]) * wide
    z_last[...] = column(basis_z[extent - 1 : extent]) * wide
    bwd[...] = jnp.zeros_like(bwd)
    load_acc[...] = jnp.zeros_like(load_acc)
    finish(copies_a)

    def load_step(h, carry):
        values = rows_in[h]
        rows, columns = row_of[h], slot_of[h]
        tops, rests = halves(values)
        left, right = [], []
        for i in range(share_rows):
            left.append(
                jnp.concatenate(
                    placed(
                        table_numbers, rows[i : i + 1], tops[i : i + 1], rests[i : i + 1]
                    ),
                    axis=0,
                )
            )
            right.append(one_hot(slot_numbers, columns[i : i + 1]))
        load_acc[...] += fast_dot(
            jnp.concatenate(left, axis=1), jnp.concatenate(right, axis=1), NT
        )
        return carry

    lax.fori_loop(0, groups, load_step, 0)
    for p in range(patches):
        load_send[p] = (
            load_acc[p * chunk : (p + 1) * chunk, :]
            + load_acc[table_rows + p * chunk : table_rows + (p + 1) * chunk, :]
        )
    copies_b = send_pencil(lambda peer: load_send.at[peer // dup], load_in, b_send, b_recv)
    load_in[pencil] = load_send[patch]
    finish(copies_b)

    sides = jnp.concatenate(
        [load_in[s, c * slab : (c + 1) * slab, :] for c in range(comps) for s in range(pencils)],
        axis=0,
    )
    fwd[...] = exact_dot(exact_dot(diag_t[...], sides, NT), diag_x[...])

    def solve_step(block, carry):
        base = pl.multiple_of(block * 8, 8)
        first = y_first[pl.ds(base, 8), :]
        last = y_last[pl.ds(base, 8), :]
        weight = y_weight[pl.ds(base, 8), :]
        side_b = fwd[pl.ds(extent + base, 8), :]
        side_c = fwd[pl.ds(2 * extent + base, 8), :]
        out_b, out_c = [None] * 8, [None] * 8
        for k in range(0, extent, 8):
            here = slice(k, k + 8)
            there = slice(3 * extent + k, 3 * extent + k + 8)
            side_a, side_d = fwd[here, :], fwd[there, :]
            weights, z_one, z_two = xz_weight[here, :], z_first[here, :], z_last[here, :]
            sum_first, sum_last = bwd[here, :], bwd[there, :]
            for i in range(8):
                row = slice(i, i + 1)
                spectral = (
                    first[row] * side_a + last[row] * side_d + side_b[row] * z_one + side_c[row] * z_two
                )
                scaled = spectral / (weights + weight[row])
                sum_first = sum_first + first[row] * scaled
                sum_last = sum_last + last[row] * scaled
                term_b, term_c = z_one * scaled, z_two * scaled
                out_b[i] = term_b if k == 0 else out_b[i] + term_b
                out_c[i] = term_c if k == 0 else out_c[i] + term_c
            bwd[here, :] = sum_first
            bwd[there, :] = sum_last
        for start, parts in ((extent, out_b), (2 * extent, out_c)):
            bwd[pl.ds(start + base, 8), :] = jnp.concatenate(
                [jnp.sum(part, axis=0, keepdims=True) for part in parts], axis=0
            )
        return carry

    lax.fori_loop(0, extent // 8, solve_step, 0)
    cells_out = exact_dot(diag_x[...], exact_dot(diag[...], bwd[...]), NT)
    for s in range(pencils):
        out_send[s] = jnp.concatenate(
            [
                cells_out[c * extent + s * slab : c * extent + (s + 1) * slab, :]
                for c in range(comps)
            ],
            axis=0,
        )
    copies_c = send_pencil(lambda peer: out_send.at[peer], out_in, c_send, c_recv)
    out_in[pencil] = out_send[pencil]
    finish(copies_c)

    for p in range(patches):
        total = out_in[p * dup]
        for u in range(1, dup):
            total = total + out_in[p * dup + u]
        top, rest_part = halves(total)
        table[p * chunk : (p + 1) * chunk, 0:slots] = top
        table[p * chunk : (p + 1) * chunk, slots : 2 * slots] = rest_part
    lookup = table[...].astype(BF16)
    places = iota((table_rows, LANES), 0).astype(F32)

    def pick_step(h, carry):
        rows, columns = row_of[h], slot_of[h]
        found = []
        for i in range(0, share_rows, 2):
            hot = jnp.concatenate(
                [
                    one_hot(slot_numbers, columns[i : i + 1]),
                    one_hot(slot_numbers, columns[i + 1 : i + 2]),
                ],
                axis=1,
            )
            both = fast_dot(lookup, jnp.concatenate([hot, hot], axis=0))
            for u in range(2):
                here = places == rows[i + u : i + u + 1]
                found.append(
                    jnp.sum(
                        jnp.where(here, both[:, u * LANES : (u + 1) * LANES], 0.0),
                        axis=0,
                        keepdims=True,
                    )
                )
        picked[h] = jnp.concatenate(found, axis=0)
        return carry

    lax.fori_loop(0, groups, pick_step, 0)

    for name in ("prim", "cidx", "inverse"):
        inputs[name].wait()
    primal = prim_ref[...]
    count = primal.shape[1]
    prim_high = lax.shift_right_logical(primal, 7)
    prim_low = jnp.bitwise_and(primal, LANES - 1)
    hot_high = jnp.where(iota((row_blocks, count), 0) == prim_high, 1.0, 0.0)
    hot_low = jnp.where(iota((LANES, count), 0) == prim_low, 1.0, 0.0)
    coarse_count = inverse_ref.shape[0]
    hot_coarse = jnp.where(iota((coarse_count, count), 0) == cidx_ref[...], 1.0, 0.0)
    flat = jnp.concatenate([picked[h] for h in range(groups)], axis=0)
    primal_values = jnp.sum(exact_dot(flat, hot_low) * hot_high, axis=0, keepdims=True)
    coarse_send[...] = exact_dot(jnp.broadcast_to(primal_values, (8, count)), hot_coarse, NT)
    copies_d = send_pencil(lambda peer: coarse_send, coarse_in, d_send, d_recv)
    coarse_in[pencil] = coarse_send[...]
    finish(copies_d)
    coarse_send2[...] = sum(coarse_in[s] for s in range(pencils))
    copies_d2 = send_group(lambda peer: coarse_send2, coarse_in2, d2_send, d2_recv)
    coarse_in2[group] = coarse_send2[...]
    finish(copies_d2)
    coarse = sum(coarse_in2[h] for h in range(groups))
    lifted = exact_dot(coarse, inverse_ref[...], NT)
    added = exact_dot(lifted, hot_coarse)[0:1]
    added_rows = exact_dot(hot_high * added, hot_low, NT)
    for h in range(groups):
        picked[h] = picked[h] + added_rows[h * share_rows : (h + 1) * share_rows, :]
    copies_e = send_group(lambda peer: picked.at[peer], owner_in, e_send, e_recv)
    owner_in[group] = picked[group]
    finish(copies_e)

    owners = jnp.concatenate([owner_in[h] for h in range(groups)], axis=0)
    top, rest_part = halves(owners)
    owner_table = jnp.concatenate([top, rest_part], axis=1).astype(BF16)

    def image_step(block, carry):
        base = pl.multiple_of(block * 8, 8)
        lane_base = pl.multiple_of(block * 8 * LANES, 8 * LANES)
        pairs = pair_ref[:, pl.ds(lane_base, 8 * LANES)]
        high = lax.shift_right_logical(pairs, 7)
        low = jnp.bitwise_and(pairs, LANES - 1).astype(F32)
        found = []
        for i in range(8):
            lanes = slice(i * LANES, (i + 1) * LANES)
            hot = jnp.concatenate(
                [one_hot(lane_numbers, low[0:1, lanes]), one_hot(lane_numbers, low[1:2, lanes])],
                axis=1,
            )
            both = fast_dot(owner_table, jnp.concatenate([hot, hot], axis=0))
            place = iota((row_blocks, LANES), 0)
            jump = jnp.where(place == high[0:1, lanes], both[:, 0:LANES], 0.0) - jnp.where(
                place == high[1:2, lanes], both[:, LANES : 2 * LANES], 0.0
            )
            found.append(jnp.sum(jump, axis=0, keepdims=True))
        image[pl.ds(base, 8), :] = jnp.concatenate(found, axis=0)
        return carry

    lax.fori_loop(0, mult_rows // 8, image_step, 0)

    for name in ("resid", "scale"):
        inputs[name].wait()
    resid, search, scale, jumps = resid_ref[...], dir_ref[...], scale_ref[...], image[...]
    scaled_resid, scaled_jump = scale * resid, scale * jumps

    def lane_sums(values):
        return jnp.sum(values, axis=0, keepdims=True)

    sums_send[...] = jnp.concatenate(
        [
            lane_sums(resid * scaled_resid),
            lane_sums(search * jumps),
            lane_sums(scaled_resid * jumps),
            lane_sums(scaled_jump * jumps),
            jnp.zeros((4, LANES), F32),
        ],
        axis=0,
    )
    copies_f = send_pencil(lambda peer: sums_send, sums_in, f_send, f_recv)
    sums_in[pencil] = sums_send[...]
    finish(copies_f)
    sums_send2[...] = sum(sums_in[s] for s in range(pencils))
    copies_f2 = send_group(lambda peer: sums_send2, sums_in2, f2_send, f2_recv)
    sums_in2[group] = sums_send2[...]
    finish(copies_f2)
    totals = jnp.sum(sum(sums_in2[h] for h in range(groups)), axis=1, keepdims=True)
    old, curvature = totals[0:1], totals[1:2]
    alpha = old / curvature
    new = old - 2.0 * alpha * totals[2:3] + alpha * (alpha * totals[3:4])
    image_out[...] = jumps
    alpha_out[...] = jnp.broadcast_to(alpha, alpha_out.shape)
    beta_out[...] = jnp.broadcast_to(new / old, beta_out.shape)


def body(
    groups,
    pencils,
    mult_iterate,
    residual,
    direction,
    mult_scale,
    eigen_basis,
    eigen_values,
    elastic_coef,
    coarse_inverse,
    send_pos,
    pair_slots,
    prim_rows,
    coarse_idx,
):
    mult_rows = direction.shape[-1] // LANES
    rows_count = send_pos.shape[-1]
    row_blocks = rows_count // LANES
    share_rows = row_blocks // groups
    patches, _, extent, _ = eigen_basis.shape
    comps = elastic_coef.shape[1]
    pairs = pair_slots.reshape(pair_slots.shape[2:])
    primal, coarse_ids = prim_rows.reshape(1, -1), coarse_idx.reshape(1, -1)
    slab = extent // pencils
    slots = 4 * extent
    width = comps * extent // (pencils // patches)
    chunk = slab * comps
    table_rows = patches * chunk
    coarse_count = coarse_inverse.shape[0]

    def vmem(*shape):
        return pltpu.VMEM(shape, F32)

    def index(*shape):
        return pltpu.VMEM(shape, jnp.int32)

    shape = (mult_rows, LANES)
    share = (groups, share_rows, LANES)
    pencil_sems = pltpu.SemaphoreType.DMA((pencils,))
    group_sems = pltpu.SemaphoreType.DMA((groups,))
    scratch = [
        vmem(2 * row_blocks, LANES),
        vmem(*share),
        vmem(*share),
        vmem(*share),
        vmem(*share),
        vmem(2 * table_rows, slots),
        vmem(patches, chunk, slots),
        vmem(pencils, chunk, slots),
        vmem(slots, slots),
        vmem(slots, slots),
        vmem(comps * extent, width),
        vmem(slots, width),
        vmem(extent, width),
        vmem(extent, width),
        vmem(extent, width),
        vmem(slots, width),
        vmem(pencils, chunk, slots),
        vmem(pencils, chunk, slots),
        vmem(table_rows, 2 * slots),
        vmem(*share),
        vmem(8, coarse_count),
        vmem(pencils, 8, coarse_count),
        vmem(8, coarse_count),
        vmem(groups, 8, coarse_count),
        vmem(*share),
        vmem(mult_rows, LANES),
        vmem(8, LANES),
        vmem(pencils, 8, LANES),
        vmem(8, LANES),
        vmem(groups, 8, LANES),
        group_sems,
        group_sems,
        pencil_sems,
        pencil_sems,
        pencil_sems,
        pencil_sems,
        pencil_sems,
        pencil_sems,
        group_sems,
        group_sems,
        group_sems,
        group_sems,
        pencil_sems,
        pencil_sems,
        group_sems,
        group_sems,
        vmem(*shape),
        vmem(*shape),
        vmem(*shape),
        vmem(*eigen_basis.shape[1:]),
        vmem(3, patches, extent),
        vmem(comps, patches, 3),
        vmem(coarse_count, coarse_count),
        index(*share),
        index(*pairs.shape),
        index(*primal.shape),
        index(*coarse_ids.shape),
        vmem(extent, width),
        vmem(extent, width),
        vmem(extent, width),
        pltpu.SemaphoreType.DMA((11,)),
    ]
    image, alpha, beta = pl.pallas_call(
        functools.partial(kernel, groups, pencils),
        out_shape=[jax.ShapeDtypeStruct(shape, F32)] * 3,
        in_specs=[pl.BlockSpec(memory_space=pltpu.HBM)] * 11,
        out_specs=[pl.BlockSpec(memory_space=pltpu.VMEM)] * 3,
        scratch_shapes=scratch,
        compiler_params=pltpu.CompilerParams(
            collective_id=0, has_side_effects=True, vmem_limit_bytes=64 * 1024 * 1024 - 65536
        ),
        name="tearing_step",
    )(
        residual.reshape(shape),
        direction.reshape(shape),
        mult_scale.reshape(shape),
        eigen_basis,
        eigen_values.transpose(1, 0, 2),
        elastic_coef.transpose(1, 0, 2),
        coarse_inverse,
        send_pos.reshape(share),
        pairs,
        primal,
        coarse_ids,
    )
    full = mult_iterate.shape
    image, alpha, beta = image.reshape(full), alpha.reshape(full), beta.reshape(full)
    next_resid = residual - alpha * image
    next_dir = mult_scale * next_resid + beta * direction
    return mult_iterate + alpha * direction, next_resid, next_dir


def solution(mesh):
    rows = P("group", "pencil", None)
    in_specs = (
        rows,
        rows,
        rows,
        rows,
        P("group", None, None, None),
        P("group", None, None),
        P("group", None, None),
        P(),
        rows,
        P("group", "pencil", None, None),
        rows,
        rows,
    )
    return jax.shard_map(
        functools.partial(body, mesh.shape["group"], mesh.shape["pencil"]),
        mesh=mesh,
        in_specs=in_specs,
        out_specs=(rows, rows, rows),
        check_vma=False,
    )
```

```python
import functools

import jax
import jax.numpy as jnp
from jax import lax
from jax.experimental import pallas as pl
from jax.experimental.pallas import tpu as pltpu
from jax.sharding import PartitionSpec as P

LANES = 128
F32 = jnp.float32
BF16 = jnp.bfloat16
HIGHEST = lax.Precision.HIGHEST
MESH = pl.DeviceIdType.MESH
NT = (((1,), (1,)), ((), ()))
NN = (((1,), (0,)), ((), ()))


def exact_dot(left, right, dims=NN):
    return lax.dot_general(left, right, dims, precision=HIGHEST, preferred_element_type=F32)


def fast_dot(left, right, dims=NN):
    return lax.dot_general(left, right, dims, preferred_element_type=F32)


def halves(values):
    top = values.astype(BF16).astype(F32)
    return top, values - top


def floor_div(values, divisor):
    return ((values.astype(F32) + 0.5) * (1.0 / divisor)).astype(jnp.int32)


def iota(shape, dim):
    return lax.broadcasted_iota(jnp.int32, shape, dim)


def column(row):
    size = row.shape[1]
    diagonal = iota((size, size), 0) == iota((size, size), 1)
    return jnp.sum(jnp.where(diagonal, row, 0.0), axis=1, keepdims=True)


def numbers(count):
    return iota((count, LANES), 0).astype(F32).astype(BF16).reshape(count // 16, 16, LANES)


def packed(row):
    return jnp.broadcast_to(row, (16, LANES)).astype(BF16)[None]


def placed(counts, row, *values):
    here = counts == packed(row)
    size = counts.shape[0] * 16
    zero = jnp.zeros((), BF16)
    return [jnp.where(here, packed(value), zero).reshape(size, LANES) for value in values]


def one_hot(counts, row):
    here = counts == packed(row)
    return jnp.where(here, jnp.ones((), BF16), jnp.zeros((), BF16)).reshape(-1, LANES)


def block_diagonal(blocks):
    total = sum(block.shape[1] for block in blocks)
    rows, before = [], 0
    for block in blocks:
        height, width = block.shape
        parts = [block]
        if before:
            parts = [jnp.zeros((height, before), F32)] + parts
        if total - before - width:
            parts = parts + [jnp.zeros((height, total - before - width), F32)]
        rows.append(jnp.concatenate(parts, axis=1) if len(parts) > 1 else block)
        before += width
    return jnp.concatenate(rows, axis=0)


def kernel(
    groups,
    pencils,
    resid_hbm,
    dir_hbm,
    scale_hbm,
    basis_hbm,
    values_hbm,
    coef_hbm,
    inverse_hbm,
    pos_hbm,
    pair_hbm,
    prim_hbm,
    cidx_hbm,
    image_out,
    alpha_out,
    beta_out,
    back_acc,
    back_send,
    rows_in,
    row_of,
    slot_of,
    load_acc,
    load_send,
    load_in,
    diag_t,
    diag,
    diag_x,
    fwd,
    y_first,
    y_last,
    y_weight,
    bwd,
    out_send,
    out_in,
    table,
    picked,
    coarse_send,
    coarse_in,
    owner_in,
    image,
    sums_send,
    sums_in,
    info_send,
    info_in,
    inverse_acc,
    hot_meets,
    meet_rows,
    meet_lanes,
    a_send,
    a_recv,
    b_send,
    b_recv,
    c_send,
    c_recv,
    d_send,
    d_recv,
    i_send,
    i_recv,
    e_send,
    e_recv,
    f_send,
    f_recv,
    resid_ref,
    dir_ref,
    scale_ref,
    basis_ref,
    values_ref,
    coef_ref,
    inverse_ref,
    pos_ref,
    pair_ref,
    prim_ref,
    cidx_ref,
    xz_weight,
    z_first,
    z_last,
    input_sem,
):
    group = lax.axis_index("group")
    pencil = lax.axis_index("pencil")
    patches, _, extent, _ = basis_hbm.shape
    comps = coef_hbm.shape[0]
    slab = extent // pencils
    share_rows = pos_ref.shape[1]
    row_blocks = groups * share_rows
    mult_rows = dir_ref.shape[0]
    slots = 4 * extent
    dup = pencils // patches
    local_i = extent // dup
    width = comps * local_i
    chunk = slab * comps
    table_rows = patches * chunk
    patch = pencil // dup
    part = lax.rem(pencil, dup)
    device = group * pencils + pencil

    def group_peer(offset):
        return lax.rem(group + offset, groups)

    def pencil_peer(offset):
        return lax.rem(pencil + offset, pencils)

    def send_group(src_of, landing, send, recv):
        copies = []
        for offset in range(1, groups):
            peer = group_peer(offset)
            copy = pltpu.make_async_remote_copy(
                src_ref=src_of(peer),
                dst_ref=landing.at[group],
                send_sem=send.at[offset],
                recv_sem=recv.at[offset],
                device_id=(peer, pencil),
                device_id_type=MESH,
            )
            copy.start()
            copies.append(copy)
        return copies

    def send_pencil(src_of, landing, send, recv):
        copies = []
        for offset in range(1, pencils):
            peer = pencil_peer(offset)
            copy = pltpu.make_async_remote_copy(
                src_ref=src_of(peer),
                dst_ref=landing.at[pencil],
                send_sem=send.at[offset],
                recv_sem=recv.at[offset],
                device_id=(group, peer),
                device_id_type=MESH,
            )
            copy.start()
            copies.append(copy)
        return copies

    def send_all(src, landing, send, recv):
        copies = []
        for g in range(groups):
            for p in range(pencils):
                if g == 0 and p == 0:
                    continue
                peer = (group_peer(g), pencil_peer(p))
                copy = pltpu.make_async_remote_copy(
                    src_ref=src,
                    dst_ref=landing.at[device],
                    send_sem=send.at[g * pencils + p],
                    recv_sem=recv.at[g * pencils + p],
                    device_id=peer,
                    device_id_type=MESH,
                )
                copy.start()
                copies.append(copy)
        landing[device] = src[...]
        return copies

    def finish(copies):
        for copy in copies:
            copy.wait_recv()
        for copy in copies:
            copy.wait_send()

    barrier = pltpu.get_barrier_semaphore()
    for g in range(groups):
        for p in range(pencils):
            if g or p:
                pl.semaphore_signal(
                    barrier,
                    inc=1,
                    device_id=(group_peer(g), pencil_peer(p)),
                    device_id_type=MESH,
                )

    inputs = {}
    for number, (name, source, target) in enumerate(
        [
            ("dir", dir_hbm, dir_ref),
            ("pair", pair_hbm, pair_ref),
            ("pos", pos_hbm, pos_ref),
            ("basis", basis_hbm.at[patch], basis_ref),
            ("values", values_hbm, values_ref),
            ("coef", coef_hbm, coef_ref),
            ("prim", prim_hbm, prim_ref),
            ("cidx", cidx_hbm, cidx_ref),
            ("inverse", inverse_hbm, inverse_ref),
            ("resid", resid_hbm, resid_ref),
            ("scale", scale_hbm, scale_ref),
        ]
    ):
        inputs[name] = pltpu.make_async_copy(source, target, input_sem.at[number])
        inputs[name].start()

    back_acc[...] = jnp.zeros_like(back_acc)
    row_numbers = numbers(row_blocks)
    lane_numbers = numbers(LANES)
    slot_numbers = numbers(slots)
    table_numbers = numbers(table_rows)
    inputs["dir"].wait()
    inputs["pair"].wait()

    def back_step(block, carry):
        base = pl.multiple_of(block * 8, 8)
        lane_base = pl.multiple_of(block * 8 * LANES, 8 * LANES)
        values = dir_ref[pl.ds(base, 8), :]
        pairs = pair_ref[:, pl.ds(lane_base, 8 * LANES)]
        high = lax.shift_right_logical(pairs, 7).astype(F32)
        low = jnp.bitwise_and(pairs, LANES - 1).astype(F32)
        tops, rests = halves(values)
        left, right = [], []
        for i in range(8):
            lanes = slice(i * LANES, (i + 1) * LANES)
            for side, sign in ((0, 1.0), (1, -1.0)):
                left.append(
                    jnp.concatenate(
                        placed(
                            row_numbers,
                            high[side : side + 1, lanes],
                            sign * tops[i : i + 1],
                            sign * rests[i : i + 1],
                        ),
                        axis=0,
                    )
                )
                right.append(one_hot(lane_numbers, low[side : side + 1, lanes]))
        back_acc[...] += fast_dot(
            jnp.concatenate(left, axis=1), jnp.concatenate(right, axis=1), NT
        )
        return carry

    lax.fori_loop(0, mult_rows // 8, back_step, 0)
    for h in range(groups):
        rows = slice(h * share_rows, (h + 1) * share_rows)
        low_rows = slice(row_blocks + h * share_rows, row_blocks + (h + 1) * share_rows)
        back_send[h] = back_acc[rows, :] + back_acc[low_rows, :]

    pl.semaphore_wait(barrier, groups * pencils - 1)
    copies_a = send_group(lambda peer: back_send.at[peer], rows_in, a_send, a_recv)
    rows_in[group] = back_send[group]

    for name in ("prim", "cidx"):
        inputs[name].wait()
    primal, coarse_ids = prim_ref[...], cidx_ref[...]
    count = primal.shape[1]
    info_send[...] = jnp.concatenate(
        [primal.astype(F32), coarse_ids.astype(F32), jnp.zeros((6, count), F32)], axis=0
    )
    copies_i = send_group(lambda peer: info_send, info_in, i_send, i_recv)
    info_in[group] = info_send[...]

    for name in ("pos", "basis", "values", "coef"):
        inputs[name].wait()
    cells = pos_ref[...]
    cycle = 4 * extent - 4
    plane = floor_div(cells, cycle)
    spot = cells - plane * cycle
    slot_of[...] = (
        spot
        + jnp.where(spot >= extent, 1, 0)
        + jnp.where(spot >= 2 * extent - 2, 2, 0)
        + jnp.where(spot >= 3 * extent - 4, 1, 0)
    ).astype(F32)
    x_index = floor_div(plane, patches * comps)
    rest = plane - x_index * (patches * comps)
    p_index = floor_div(rest, comps)
    c_index = rest - p_index * comps
    row_of[...] = (p_index * chunk + c_index * slab + x_index).astype(F32)

    basis_x = basis_ref[0]
    basis_y = basis_ref[1]
    basis_z = basis_ref[2]

    def of_patch(ref, row):
        return sum(jnp.where(patch == p, ref[row, p : p + 1, :], 0.0) for p in range(patches))

    spectrum = [of_patch(values_ref, axis) for axis in range(3)]
    coef = [of_patch(coef_ref, c) for c in range(comps)]
    along_x = spectrum[0]
    if dup > 1:
        basis_x = sum(
            jnp.where(part == u, basis_x[:, u * local_i : (u + 1) * local_i], 0.0)
            for u in range(dup)
        )
        along_x = sum(
            jnp.where(part == u, along_x[:, u * local_i : (u + 1) * local_i], 0.0)
            for u in range(dup)
        )
    diag[...] = block_diagonal([basis_z, basis_y, basis_y, basis_z])
    basis_yt, basis_zt = basis_y.T, basis_z.T
    diag_t[...] = block_diagonal([basis_zt, basis_yt, basis_yt, basis_zt])
    diag_x[...] = block_diagonal([basis_x] * comps)
    ones = jnp.ones((1, local_i), F32)
    weight_x = jnp.concatenate([coef[c][:, 0:1] * along_x for c in range(comps)], axis=1)
    weight_y = jnp.concatenate([coef[c][:, 1:2] * ones for c in range(comps)], axis=1)
    weight_z = jnp.concatenate([coef[c][:, 2:3] * ones for c in range(comps)], axis=1)
    y_weight[...] = column(spectrum[1]) * weight_y
    wide = jnp.ones((1, width), F32)
    y_first[...] = column(basis_y[0:1]) * wide
    y_last[...] = column(basis_y[extent - 1 : extent]) * wide
    xz_weight[...] = weight_x + column(spectrum[2]) * weight_z
    z_first[...] = column(basis_z[0:1]) * wide
    z_last[...] = column(basis_z[extent - 1 : extent]) * wide
    bwd[...] = jnp.zeros_like(bwd)
    load_acc[...] = jnp.zeros_like(load_acc)

    inverse_acc[...] = jnp.zeros_like(inverse_acc)
    lane_of = iota((1, LANES), 1).astype(F32)

    def inverse_step(block, carry):
        lane_base = pl.multiple_of(block * 8 * LANES, 8 * LANES)
        pairs = pair_ref[:, pl.ds(lane_base, 8 * LANES)]
        high = lax.shift_right_logical(pairs, 7).astype(F32)
        low = jnp.bitwise_and(pairs, LANES - 1).astype(F32)
        first = jnp.zeros((1, LANES), F32) + (block * 8 + 1).astype(F32)
        left, right = [], []
        for i in range(8):
            lanes = slice(i * LANES, (i + 1) * LANES)
            for side, sign in ((0, 1.0), (1, -1.0)):
                left.append(
                    jnp.concatenate(
                        placed(
                            row_numbers, high[side : side + 1, lanes], sign * (first + i), lane_of
                        ),
                        axis=0,
                    )
                )
                right.append(one_hot(lane_numbers, low[side : side + 1, lanes]))
        inverse_acc[...] += fast_dot(
            jnp.concatenate(left, axis=1), jnp.concatenate(right, axis=1), NT
        )
        return carry

    lax.fori_loop(0, mult_rows // 8, inverse_step, 0)
    finish(copies_a)

    def load_step(h, carry):
        values = rows_in[h]
        rows, columns = row_of[h], slot_of[h]
        tops, rests = halves(values)
        left, right = [], []
        for i in range(share_rows):
            left.append(
                jnp.concatenate(
                    placed(
                        table_numbers, rows[i : i + 1], tops[i : i + 1], rests[i : i + 1]
                    ),
                    axis=0,
                )
            )
            right.append(one_hot(slot_numbers, columns[i : i + 1]))
        load_acc[...] += fast_dot(
            jnp.concatenate(left, axis=1), jnp.concatenate(right, axis=1), NT
        )
        return carry

    lax.fori_loop(0, groups, load_step, 0)
    for p in range(patches):
        load_send[p] = (
            load_acc[p * chunk : (p + 1) * chunk, :]
            + load_acc[table_rows + p * chunk : table_rows + (p + 1) * chunk, :]
        )
    copies_b = send_pencil(lambda peer: load_send.at[peer // dup], load_in, b_send, b_recv)
    load_in[pencil] = load_send[patch]

    finish(copies_i)
    all_rows = jnp.concatenate([info_in[h, 0:1, :] for h in range(groups)], axis=1)
    all_ids = jnp.concatenate([info_in[h, 1:2, :] for h in range(groups)], axis=1)
    owner = jnp.concatenate([jnp.full((1, count), h, F32) for h in range(groups)], axis=1)
    share = share_rows * LANES
    local = all_rows - (group * share).astype(F32)
    mine = jnp.logical_and(local >= 0.0, local < share)
    line = jnp.floor(local * (1.0 / LANES))
    met_high = jnp.where(mine, owner * share_rows + line, -1.0)
    met_low = local - line * LANES

    def numbered(size):
        return iota((size, groups * count), 0).astype(F32)

    met_hot = jnp.where(numbered(LANES) == met_low, 1.0, 0.0).astype(BF16)
    met_values = fast_dot(inverse_acc[...].astype(BF16), met_hot)
    met_here = numbered(row_blocks) == met_high
    met_row = jnp.sum(
        jnp.where(met_here, met_values[0:row_blocks], 0.0), axis=0, keepdims=True
    )
    met_lane = jnp.sum(
        jnp.where(met_here, met_values[row_blocks : 2 * row_blocks], 0.0), axis=0, keepdims=True
    )
    meet_rows[...] = jnp.where(
        numbered(mult_rows) == jnp.abs(met_row) - 1.0, jnp.where(met_row > 0.0, 1.0, -1.0), 0.0
    )
    meet_lanes[...] = jnp.where(numbered(LANES) == met_lane, 1.0, 0.0)
    coarse_count = inverse_hbm.shape[0]
    hot_meets[...] = jnp.where(numbered(coarse_count) == all_ids, 1.0, 0.0)
    finish(copies_b)

    sides = jnp.concatenate(
        [load_in[s, c * slab : (c + 1) * slab, :] for c in range(comps) for s in range(pencils)],
        axis=0,
    )
    fwd[...] = exact_dot(exact_dot(diag_t[...], sides, NT), diag_x[...])

    def solve_step(block, carry):
        base = pl.multiple_of(block * 8, 8)
        first = y_first[pl.ds(base, 8), :]
        last = y_last[pl.ds(base, 8), :]
        weight = y_weight[pl.ds(base, 8), :]
        side_b = fwd[pl.ds(extent + base, 8), :]
        side_c = fwd[pl.ds(2 * extent + base, 8), :]
        out_b, out_c = [None] * 8, [None] * 8
        for k in range(0, extent, 8):
            here = slice(k, k + 8)
            there = slice(3 * extent + k, 3 * extent + k + 8)
            side_a, side_d = fwd[here, :], fwd[there, :]
            weights, z_one, z_two = xz_weight[here, :], z_first[here, :], z_last[here, :]
            sum_first, sum_last = bwd[here, :], bwd[there, :]
            for i in range(8):
                row = slice(i, i + 1)
                spectral = (
                    first[row] * side_a + last[row] * side_d + side_b[row] * z_one + side_c[row] * z_two
                )
                scaled = spectral / (weights + weight[row])
                sum_first = sum_first + first[row] * scaled
                sum_last = sum_last + last[row] * scaled
                term_b, term_c = z_one * scaled, z_two * scaled
                out_b[i] = term_b if k == 0 else out_b[i] + term_b
                out_c[i] = term_c if k == 0 else out_c[i] + term_c
            bwd[here, :] = sum_first
            bwd[there, :] = sum_last
        for start, parts in ((extent, out_b), (2 * extent, out_c)):
            bwd[pl.ds(start + base, 8), :] = jnp.concatenate(
                [jnp.sum(part, axis=0, keepdims=True) for part in parts], axis=0
            )
        return carry

    lax.fori_loop(0, extent // 8, solve_step, 0)
    cells_out = exact_dot(diag_x[...], exact_dot(diag[...], bwd[...]), NT)
    for s in range(pencils):
        out_send[s] = jnp.concatenate(
            [
                cells_out[c * extent + s * slab : c * extent + (s + 1) * slab, :]
                for c in range(comps)
            ],
            axis=0,
        )
    copies_c = send_pencil(lambda peer: out_send.at[peer], out_in, c_send, c_recv)
    out_in[pencil] = out_send[pencil]
    finish(copies_c)

    for p in range(patches):
        total = out_in[p * dup]
        for u in range(1, dup):
            total = total + out_in[p * dup + u]
        top, rest_part = halves(total)
        table[p * chunk : (p + 1) * chunk, 0:slots] = top
        table[p * chunk : (p + 1) * chunk, slots : 2 * slots] = rest_part
    lookup = table[...].astype(BF16)
    places = iota((table_rows, LANES), 0).astype(F32)

    def pick_step(h, carry):
        rows, columns = row_of[h], slot_of[h]
        found = []
        for i in range(0, share_rows, 2):
            hot = jnp.concatenate(
                [
                    one_hot(slot_numbers, columns[i : i + 1]),
                    one_hot(slot_numbers, columns[i + 1 : i + 2]),
                ],
                axis=1,
            )
            both = fast_dot(lookup, jnp.concatenate([hot, hot], axis=0))
            for u in range(2):
                here = places == rows[i + u : i + u + 1]
                found.append(
                    jnp.sum(
                        jnp.where(here, both[:, u * LANES : (u + 1) * LANES], 0.0),
                        axis=0,
                        keepdims=True,
                    )
                )
        picked[h] = jnp.concatenate(found, axis=0)
        return carry

    lax.fori_loop(0, groups, pick_step, 0)

    copies_e = send_group(lambda peer: picked.at[peer], owner_in, e_send, e_recv)
    owner_in[group] = picked[group]
    prim_high = lax.shift_right_logical(primal, 7)
    prim_low = jnp.bitwise_and(primal, LANES - 1)
    hot_high = jnp.where(iota((row_blocks, count), 0) == prim_high, 1.0, 0.0)
    hot_low = jnp.where(iota((LANES, count), 0) == prim_low, 1.0, 0.0)
    hot_coarse = jnp.where(iota((coarse_count, count), 0) == coarse_ids, 1.0, 0.0)
    flat = jnp.concatenate([picked[h] for h in range(groups)], axis=0)
    primal_values = jnp.sum(exact_dot(flat, hot_low) * hot_high, axis=0, keepdims=True)
    coarse_send[...] = exact_dot(jnp.broadcast_to(primal_values, (8, count)), hot_coarse, NT)[0:1]
    copies_d = send_all(coarse_send, coarse_in, d_send, d_recv)
    finish(copies_e)

    owners = jnp.concatenate([owner_in[h] for h in range(groups)], axis=0)
    top, rest_part = halves(owners)
    owner_table = jnp.concatenate([top, rest_part], axis=1).astype(BF16)

    def image_step(block, carry):
        base = pl.multiple_of(block * 8, 8)
        lane_base = pl.multiple_of(block * 8 * LANES, 8 * LANES)
        pairs = pair_ref[:, pl.ds(lane_base, 8 * LANES)]
        high = lax.shift_right_logical(pairs, 7)
        low = jnp.bitwise_and(pairs, LANES - 1).astype(F32)
        found = []
        for i in range(8):
            lanes = slice(i * LANES, (i + 1) * LANES)
            hot = jnp.concatenate(
                [one_hot(lane_numbers, low[0:1, lanes]), one_hot(lane_numbers, low[1:2, lanes])],
                axis=1,
            )
            both = fast_dot(owner_table, jnp.concatenate([hot, hot], axis=0))
            place = iota((row_blocks, LANES), 0)
            jump = jnp.where(place == high[0:1, lanes], both[:, 0:LANES], 0.0) - jnp.where(
                place == high[1:2, lanes], both[:, LANES : 2 * LANES], 0.0
            )
            found.append(jnp.sum(jump, axis=0, keepdims=True))
        image[pl.ds(base, 8), :] = jnp.concatenate(found, axis=0)
        return carry

    lax.fori_loop(0, mult_rows // 8, image_step, 0)

    inputs["inverse"].wait()
    finish(copies_d)
    coarse = sum(coarse_in[d] for d in range(groups * pencils))
    lifted = exact_dot(jnp.broadcast_to(coarse, (8, coarse_count)), inverse_ref[...], NT)
    lifts = exact_dot(lifted, hot_meets[...])[0:1]
    jump_lift = exact_dot(meet_rows[...] * lifts, meet_lanes[...], NT)

    for name in ("resid", "scale"):
        inputs[name].wait()
    resid, search, scale, jumps = resid_ref[...], dir_ref[...], scale_ref[...], image[...] + jump_lift
    scaled_resid, scaled_jump = scale * resid, scale * jumps

    def total_of(values):
        return jnp.sum(jnp.sum(values, axis=0, keepdims=True), axis=1, keepdims=True)

    parts = [
        total_of(resid * scaled_resid),
        total_of(search * jumps),
        total_of(scaled_resid * jumps),
        total_of(scaled_jump * jumps),
    ]
    lane = iota((1, LANES), 1)
    sums_send[...] = sum(jnp.where(lane == n, value, 0.0) for n, value in enumerate(parts))
    finish(send_all(sums_send, sums_in, f_send, f_recv))
    sums = sum(sums_in[d] for d in range(groups * pencils))
    totals = [sums[:, n : n + 1] for n in range(4)]
    old, curvature = totals[0], totals[1]
    alpha = old / curvature
    new = old - 2.0 * alpha * totals[2] + alpha * (alpha * totals[3])
    image_out[...] = jumps
    alpha_out[...] = jnp.broadcast_to(alpha, alpha_out.shape)
    beta_out[...] = jnp.broadcast_to(new / old, beta_out.shape)


def body(
    groups,
    pencils,
    mult_iterate,
    residual,
    direction,
    mult_scale,
    eigen_basis,
    eigen_values,
    elastic_coef,
    coarse_inverse,
    send_pos,
    pair_slots,
    prim_rows,
    coarse_idx,
):
    mult_rows = direction.shape[-1] // LANES
    rows_count = send_pos.shape[-1]
    row_blocks = rows_count // LANES
    share_rows = row_blocks // groups
    patches, _, extent, _ = eigen_basis.shape
    comps = elastic_coef.shape[1]
    pairs = pair_slots.reshape(pair_slots.shape[2:])
    primal, coarse_ids = prim_rows.reshape(1, -1), coarse_idx.reshape(1, -1)
    slab = extent // pencils
    slots = 4 * extent
    width = comps * extent // (pencils // patches)
    chunk = slab * comps
    table_rows = patches * chunk
    coarse_count = coarse_inverse.shape[0]
    primal_count = primal.shape[1]
    devices = groups * pencils

    def vmem(*shape):
        return pltpu.VMEM(shape, F32)

    def index(*shape):
        return pltpu.VMEM(shape, jnp.int32)

    shape = (mult_rows, LANES)
    share = (groups, share_rows, LANES)
    pencil_sems = pltpu.SemaphoreType.DMA((pencils,))
    device_sems = pltpu.SemaphoreType.DMA((devices,))
    group_sems = pltpu.SemaphoreType.DMA((groups,))
    scratch = [
        vmem(2 * row_blocks, LANES),
        vmem(*share),
        vmem(*share),
        vmem(*share),
        vmem(*share),
        vmem(2 * table_rows, slots),
        vmem(patches, chunk, slots),
        vmem(pencils, chunk, slots),
        vmem(slots, slots),
        vmem(slots, slots),
        vmem(comps * extent, width),
        vmem(slots, width),
        vmem(extent, width),
        vmem(extent, width),
        vmem(extent, width),
        vmem(slots, width),
        vmem(pencils, chunk, slots),
        vmem(pencils, chunk, slots),
        vmem(table_rows, 2 * slots),
        vmem(*share),
        vmem(1, coarse_count),
        vmem(devices, 1, coarse_count),
        vmem(*share),
        vmem(mult_rows, LANES),
        vmem(1, LANES),
        vmem(devices, 1, LANES),
        vmem(8, primal_count),
        vmem(groups, 8, primal_count),
        vmem(2 * row_blocks, LANES),
        vmem(coarse_count, groups * primal_count),
        vmem(mult_rows, groups * primal_count),
        vmem(LANES, groups * primal_count),
        group_sems,
        group_sems,
        pencil_sems,
        pencil_sems,
        pencil_sems,
        pencil_sems,
        device_sems,
        device_sems,
        group_sems,
        group_sems,
        group_sems,
        group_sems,
        device_sems,
        device_sems,
        vmem(*shape),
        vmem(*shape),
        vmem(*shape),
        vmem(*eigen_basis.shape[1:]),
        vmem(3, patches, extent),
        vmem(comps, patches, 3),
        vmem(coarse_count, coarse_count),
        index(*share),
        index(*pairs.shape),
        index(*primal.shape),
        index(*coarse_ids.shape),
        vmem(extent, width),
        vmem(extent, width),
        vmem(extent, width),
        pltpu.SemaphoreType.DMA((11,)),
    ]
    image, alpha, beta = pl.pallas_call(
        functools.partial(kernel, groups, pencils),
        out_shape=[jax.ShapeDtypeStruct(shape, F32)] * 3,
        in_specs=[pl.BlockSpec(memory_space=pltpu.HBM)] * 11,
        out_specs=[pl.BlockSpec(memory_space=pltpu.VMEM)] * 3,
        scratch_shapes=scratch,
        compiler_params=pltpu.CompilerParams(
            collective_id=0, has_side_effects=True, vmem_limit_bytes=64 * 1024 * 1024 - 65536
        ),
        name="tearing_step",
    )(
        residual.reshape(shape),
        direction.reshape(shape),
        mult_scale.reshape(shape),
        eigen_basis,
        eigen_values.transpose(1, 0, 2),
        elastic_coef.transpose(1, 0, 2),
        coarse_inverse,
        send_pos.reshape(share),
        pairs,
        primal,
        coarse_ids,
    )
    full = mult_iterate.shape
    image, alpha, beta = image.reshape(full), alpha.reshape(full), beta.reshape(full)
    next_resid = residual - alpha * image
    next_dir = mult_scale * next_resid + beta * direction
    return mult_iterate + alpha * direction, next_resid, next_dir


def solution(mesh):
    rows = P("group", "pencil", None)
    in_specs = (
        rows,
        rows,
        rows,
        rows,
        P("group", None, None, None),
        P("group", None, None),
        P("group", None, None),
        P(),
        rows,
        P("group", "pencil", None, None),
        rows,
        rows,
    )
    return jax.shard_map(
        functools.partial(body, mesh.shape["group"], mesh.shape["pencil"]),
        mesh=mesh,
        in_specs=in_specs,
        out_specs=(rows, rows, rows),
        check_vma=False,
    )
```

```python
import functools

import jax
import jax.numpy as jnp
from jax import lax
from jax.experimental import pallas as pl
from jax.experimental.pallas import tpu as pltpu
from jax.sharding import PartitionSpec as P

LANES = 128
F32 = jnp.float32
BF16 = jnp.bfloat16
MESH = pl.DeviceIdType.MESH
NT = (((1,), (1,)), ((), ()))
NN = (((1,), (0,)), ((), ()))


def fast_dot(left, right, dims=NN):
    return lax.dot_general(left, right, dims, preferred_element_type=F32)


def halves(values):
    top = values.astype(BF16).astype(F32)
    return top, values - top


def split_dot(left, right, dims=NN):
    left_top, left_rest = (half.astype(BF16) for half in halves(left))
    right_top, right_rest = (half.astype(BF16) for half in halves(right))
    return (
        fast_dot(left_top, right_top, dims)
        + fast_dot(left_top, right_rest, dims)
        + fast_dot(left_rest, right_top, dims)
    )


def hot_dot(left, right, dims=NN):
    top, rest = (half.astype(BF16) for half in halves(left))
    hot = right.astype(BF16)
    return fast_dot(top, hot, dims) + fast_dot(rest, hot, dims)


def floor_div(values, divisor):
    return ((values.astype(F32) + 0.5) * (1.0 / divisor)).astype(jnp.int32)


def iota(shape, dim):
    return lax.broadcasted_iota(jnp.int32, shape, dim)


def column(row):
    size = row.shape[1]
    diagonal = iota((size, size), 0) == iota((size, size), 1)
    return jnp.sum(jnp.where(diagonal, row, 0.0), axis=1, keepdims=True)


def numbers(count):
    return iota((count, LANES), 0).astype(F32).astype(BF16).reshape(count // 16, 16, LANES)


def packed(row):
    return jnp.broadcast_to(row, (16, LANES)).astype(BF16)[None]


def placed(counts, row, *values):
    here = counts == packed(row)
    size = counts.shape[0] * 16
    zero = jnp.zeros((), BF16)
    return [jnp.where(here, packed(value), zero).reshape(size, LANES) for value in values]


def one_hot(counts, row):
    here = counts == packed(row)
    return jnp.where(here, jnp.ones((), BF16), jnp.zeros((), BF16)).reshape(-1, LANES)


def block_diagonal(blocks):
    total = sum(block.shape[1] for block in blocks)
    rows, before = [], 0
    for block in blocks:
        height, width = block.shape
        parts = [block]
        if before:
            parts = [jnp.zeros((height, before), F32)] + parts
        if total - before - width:
            parts = parts + [jnp.zeros((height, total - before - width), F32)]
        rows.append(jnp.concatenate(parts, axis=1) if len(parts) > 1 else block)
        before += width
    return jnp.concatenate(rows, axis=0)


def kernel(
    groups,
    pencils,
    resid_hbm,
    dir_hbm,
    scale_hbm,
    basis_hbm,
    values_hbm,
    coef_hbm,
    inverse_hbm,
    pos_hbm,
    pair_hbm,
    prim_hbm,
    cidx_hbm,
    image_out,
    alpha_out,
    beta_out,
    back_acc,
    back_send,
    rows_in,
    row_of,
    slot_of,
    load_acc,
    load_send,
    load_in,
    diag_t,
    diag,
    diag_x,
    fwd,
    y_first,
    y_last,
    y_weight,
    bwd,
    out_send,
    out_in,
    table,
    picked,
    coarse_send,
    coarse_in,
    owner_in,
    image,
    sums_send,
    sums_in,
    info_send,
    info_in,
    inverse_acc,
    hot_meets,
    meet_rows,
    meet_lanes,
    a_send,
    a_recv,
    b_send,
    b_recv,
    c_send,
    c_recv,
    d_send,
    d_recv,
    i_send,
    i_recv,
    e_send,
    e_recv,
    f_send,
    f_recv,
    resid_ref,
    dir_ref,
    scale_ref,
    basis_ref,
    values_ref,
    coef_ref,
    inverse_ref,
    pos_ref,
    pair_ref,
    prim_ref,
    cidx_ref,
    xz_weight,
    z_first,
    z_last,
    input_sem,
):
    group = lax.axis_index("group")
    pencil = lax.axis_index("pencil")
    patches, _, extent, _ = basis_hbm.shape
    comps = coef_hbm.shape[0]
    slab = extent // pencils
    share_rows = pos_ref.shape[1]
    row_blocks = groups * share_rows
    mult_rows = dir_ref.shape[0]
    slots = 4 * extent
    dup = pencils // patches
    local_i = extent // dup
    width = comps * local_i
    chunk = slab * comps
    table_rows = patches * chunk
    patch = pencil // dup
    part = lax.rem(pencil, dup)
    device = group * pencils + pencil

    def group_peer(offset):
        return lax.rem(group + offset, groups)

    def pencil_peer(offset):
        return lax.rem(pencil + offset, pencils)

    def group_copy(src, landing, send, recv, offset, peer):
        return pltpu.make_async_remote_copy(
            src_ref=src,
            dst_ref=landing.at[group],
            send_sem=send.at[offset],
            recv_sem=recv.at[offset],
            device_id=(peer, pencil),
            device_id_type=MESH,
        )

    def send_group(src_of, landing, send, recv):
        copies = []
        for offset in range(1, groups):
            peer = group_peer(offset)
            copy = group_copy(src_of(peer), landing, send, recv, offset, peer)
            copy.start()
            copies.append(copy)
        return copies

    def send_pencil(src_of, landing, send, recv):
        copies = []
        for offset in range(1, pencils):
            peer = pencil_peer(offset)
            copy = pltpu.make_async_remote_copy(
                src_ref=src_of(peer),
                dst_ref=landing.at[pencil],
                send_sem=send.at[offset],
                recv_sem=recv.at[offset],
                device_id=(group, peer),
                device_id_type=MESH,
            )
            copy.start()
            copies.append(copy)
        return copies

    def send_all(src, landing, send, recv):
        copies = []
        for g in range(groups):
            for p in range(pencils):
                if g == 0 and p == 0:
                    continue
                peer = (group_peer(g), pencil_peer(p))
                copy = pltpu.make_async_remote_copy(
                    src_ref=src,
                    dst_ref=landing.at[device],
                    send_sem=send.at[g * pencils + p],
                    recv_sem=recv.at[g * pencils + p],
                    device_id=peer,
                    device_id_type=MESH,
                )
                copy.start()
                copies.append(copy)
        landing[device] = src[...]
        return copies

    def finish(copies):
        for copy in copies:
            copy.wait_recv()
        for copy in copies:
            copy.wait_send()

    barrier = pltpu.get_barrier_semaphore()
    for g in range(groups):
        for p in range(pencils):
            if g or p:
                pl.semaphore_signal(
                    barrier,
                    inc=1,
                    device_id=(group_peer(g), pencil_peer(p)),
                    device_id_type=MESH,
                )

    inputs = {}
    for number, (name, source, target) in enumerate(
        [
            ("dir", dir_hbm, dir_ref),
            ("pair", pair_hbm, pair_ref),
            ("pos", pos_hbm, pos_ref),
            ("basis", basis_hbm.at[patch], basis_ref),
            ("values", values_hbm, values_ref),
            ("coef", coef_hbm, coef_ref),
            ("prim", prim_hbm, prim_ref),
            ("cidx", cidx_hbm, cidx_ref),
            ("inverse", inverse_hbm, inverse_ref),
            ("resid", resid_hbm, resid_ref),
            ("scale", scale_hbm, scale_ref),
        ]
    ):
        inputs[name] = pltpu.make_async_copy(source, target, input_sem.at[number])
        inputs[name].start()

    back_acc[...] = jnp.zeros_like(back_acc)
    row_numbers = numbers(row_blocks)
    lane_numbers = numbers(LANES)
    slot_numbers = numbers(slots)
    table_numbers = numbers(table_rows)
    inputs["dir"].wait()
    inputs["pair"].wait()

    def back_step(block, carry):
        base = pl.multiple_of(block * 8, 8)
        lane_base = pl.multiple_of(block * 8 * LANES, 8 * LANES)
        values = dir_ref[pl.ds(base, 8), :]
        pairs = pair_ref[:, pl.ds(lane_base, 8 * LANES)]
        high = lax.shift_right_logical(pairs, 7).astype(F32)
        low = jnp.bitwise_and(pairs, LANES - 1).astype(F32)
        tops, rests = halves(values)
        left, right = [], []
        for i in range(8):
            lanes = slice(i * LANES, (i + 1) * LANES)
            for side, sign in ((0, 1.0), (1, -1.0)):
                left.append(
                    jnp.concatenate(
                        placed(
                            row_numbers,
                            high[side : side + 1, lanes],
                            sign * tops[i : i + 1],
                            sign * rests[i : i + 1],
                        ),
                        axis=0,
                    )
                )
                right.append(one_hot(lane_numbers, low[side : side + 1, lanes]))
        back_acc[...] += fast_dot(
            jnp.concatenate(left, axis=1), jnp.concatenate(right, axis=1), NT
        )
        return carry

    lax.fori_loop(0, mult_rows // 8, back_step, 0)
    for h in range(groups):
        rows = slice(h * share_rows, (h + 1) * share_rows)
        low_rows = slice(row_blocks + h * share_rows, row_blocks + (h + 1) * share_rows)
        back_send[h] = back_acc[rows, :] + back_acc[low_rows, :]

    pl.semaphore_wait(barrier, groups * pencils - 1)
    copies_a = send_group(lambda peer: back_send.at[peer], rows_in, a_send, a_recv)
    rows_in[group] = back_send[group]

    for name in ("prim", "cidx"):
        inputs[name].wait()
    primal, coarse_ids = prim_ref[...], cidx_ref[...]
    count = primal.shape[1]
    info_send[...] = jnp.concatenate(
        [primal.astype(F32), coarse_ids.astype(F32), jnp.zeros((6, count), F32)], axis=0
    )
    copies_i = send_group(lambda peer: info_send, info_in, i_send, i_recv)
    info_in[group] = info_send[...]

    inputs["pos"].wait()
    cells = pos_ref[...]
    cycle = 4 * extent - 4
    plane = floor_div(cells, cycle)
    spot = cells - plane * cycle
    slot_of[...] = (
        spot
        + jnp.where(spot >= extent, 1, 0)
        + jnp.where(spot >= 2 * extent - 2, 2, 0)
        + jnp.where(spot >= 3 * extent - 4, 1, 0)
    ).astype(F32)
    x_index = floor_div(plane, patches * comps)
    rest = plane - x_index * (patches * comps)
    p_index = floor_div(rest, comps)
    c_index = rest - p_index * comps
    row_of[...] = (p_index * chunk + c_index * slab + x_index).astype(F32)

    load_acc[...] = jnp.zeros_like(load_acc)


    def load_step(offset, carry):
        h = lax.rem(group - offset + groups, groups)
        group_copy(back_send.at[h], rows_in, a_send, a_recv, offset, h).wait_recv()
        load_from(h)
        return carry

    def load_from(h):
        values = rows_in[h]
        rows, columns = row_of[h], slot_of[h]
        tops, rests = halves(values)
        left, right = [], []
        for i in range(share_rows):
            left.append(
                jnp.concatenate(
                    placed(
                        table_numbers, rows[i : i + 1], tops[i : i + 1], rests[i : i + 1]
                    ),
                    axis=0,
                )
            )
            right.append(one_hot(slot_numbers, columns[i : i + 1]))
        load_acc[...] += fast_dot(
            jnp.concatenate(left, axis=1), jnp.concatenate(right, axis=1), NT
        )

    load_from(group)
    lax.fori_loop(1, groups, load_step, 0)
    for copy in copies_a:
        copy.wait_send()
    for p in range(patches):
        load_send[p] = (
            load_acc[p * chunk : (p + 1) * chunk, :]
            + load_acc[table_rows + p * chunk : table_rows + (p + 1) * chunk, :]
        )
    copies_b = send_pencil(lambda peer: load_send.at[peer // dup], load_in, b_send, b_recv)
    load_in[pencil] = load_send[patch]

    for name in ("basis", "values", "coef"):
        inputs[name].wait()
    basis_x = basis_ref[0]
    basis_y = basis_ref[1]
    basis_z = basis_ref[2]

    def of_patch(ref, row):
        return sum(jnp.where(patch == p, ref[row, p : p + 1, :], 0.0) for p in range(patches))

    spectrum = [of_patch(values_ref, axis) for axis in range(3)]
    coef = [of_patch(coef_ref, c) for c in range(comps)]
    along_x = spectrum[0]
    if dup > 1:
        basis_x = sum(
            jnp.where(part == u, basis_x[:, u * local_i : (u + 1) * local_i], 0.0)
            for u in range(dup)
        )
        along_x = sum(
            jnp.where(part == u, along_x[:, u * local_i : (u + 1) * local_i], 0.0)
            for u in range(dup)
        )
    diag[...] = block_diagonal([basis_z, basis_y, basis_y, basis_z])
    basis_yt, basis_zt = basis_y.T, basis_z.T
    diag_t[...] = block_diagonal([basis_zt, basis_yt, basis_yt, basis_zt])
    diag_x[...] = block_diagonal([basis_x] * comps)
    ones = jnp.ones((1, local_i), F32)
    weight_x = jnp.concatenate([coef[c][:, 0:1] * along_x for c in range(comps)], axis=1)
    weight_y = jnp.concatenate([coef[c][:, 1:2] * ones for c in range(comps)], axis=1)
    weight_z = jnp.concatenate([coef[c][:, 2:3] * ones for c in range(comps)], axis=1)
    y_weight[...] = column(spectrum[1]) * weight_y
    wide = jnp.ones((1, width), F32)
    y_first[...] = column(basis_y[0:1]) * wide
    y_last[...] = column(basis_y[extent - 1 : extent]) * wide
    xz_weight[...] = weight_x + column(spectrum[2]) * weight_z
    z_first[...] = column(basis_z[0:1]) * wide
    z_last[...] = column(basis_z[extent - 1 : extent]) * wide
    bwd[...] = jnp.zeros_like(bwd)
    inverse_acc[...] = jnp.zeros_like(inverse_acc)
    lane_of = iota((1, LANES), 1).astype(F32)

    def inverse_step(block, carry):
        lane_base = pl.multiple_of(block * 8 * LANES, 8 * LANES)
        pairs = pair_ref[:, pl.ds(lane_base, 8 * LANES)]
        high = lax.shift_right_logical(pairs, 7).astype(F32)
        low = jnp.bitwise_and(pairs, LANES - 1).astype(F32)
        first = jnp.zeros((1, LANES), F32) + (block * 8 + 1).astype(F32)
        left, right = [], []
        for i in range(8):
            lanes = slice(i * LANES, (i + 1) * LANES)
            for side, sign in ((0, 1.0), (1, -1.0)):
                left.append(
                    jnp.concatenate(
                        placed(
                            row_numbers, high[side : side + 1, lanes], sign * (first + i), lane_of
                        ),
                        axis=0,
                    )
                )
                right.append(one_hot(lane_numbers, low[side : side + 1, lanes]))
        inverse_acc[...] += fast_dot(
            jnp.concatenate(left, axis=1), jnp.concatenate(right, axis=1), NT
        )
        return carry

    lax.fori_loop(0, mult_rows // 8, inverse_step, 0)
    finish(copies_b)

    sides = jnp.concatenate(
        [load_in[s, c * slab : (c + 1) * slab, :] for c in range(comps) for s in range(pencils)],
        axis=0,
    )
    fwd[...] = split_dot(split_dot(diag_t[...], sides, NT), diag_x[...])

    def solve_step(block, carry):
        base = pl.multiple_of(block * 8, 8)
        first = y_first[pl.ds(base, 8), :]
        last = y_last[pl.ds(base, 8), :]
        weight = y_weight[pl.ds(base, 8), :]
        side_b = fwd[pl.ds(extent + base, 8), :]
        side_c = fwd[pl.ds(2 * extent + base, 8), :]
        out_b, out_c = [None] * 8, [None] * 8
        for k in range(0, extent, 8):
            here = slice(k, k + 8)
            there = slice(3 * extent + k, 3 * extent + k + 8)
            side_a, side_d = fwd[here, :], fwd[there, :]
            weights, z_one, z_two = xz_weight[here, :], z_first[here, :], z_last[here, :]
            sum_first, sum_last = bwd[here, :], bwd[there, :]
            for i in range(8):
                row = slice(i, i + 1)
                spectral = (
                    first[row] * side_a + last[row] * side_d + side_b[row] * z_one + side_c[row] * z_two
                )
                scaled = spectral / (weights + weight[row])
                sum_first = sum_first + first[row] * scaled
                sum_last = sum_last + last[row] * scaled
                term_b, term_c = z_one * scaled, z_two * scaled
                out_b[i] = term_b if k == 0 else out_b[i] + term_b
                out_c[i] = term_c if k == 0 else out_c[i] + term_c
            bwd[here, :] = sum_first
            bwd[there, :] = sum_last
        for start, parts in ((extent, out_b), (2 * extent, out_c)):
            bwd[pl.ds(start + base, 8), :] = jnp.concatenate(
                [jnp.sum(part, axis=0, keepdims=True) for part in parts], axis=0
            )
        return carry

    lax.fori_loop(0, extent // 8, solve_step, 0)
    cells_out = split_dot(diag_x[...], split_dot(diag[...], bwd[...]), NT)
    for s in range(pencils):
        out_send[s] = jnp.concatenate(
            [
                cells_out[c * extent + s * slab : c * extent + (s + 1) * slab, :]
                for c in range(comps)
            ],
            axis=0,
        )
    copies_c = send_pencil(lambda peer: out_send.at[peer], out_in, c_send, c_recv)
    out_in[pencil] = out_send[pencil]
    finish(copies_i)
    all_rows = jnp.concatenate([info_in[h, 0:1, :] for h in range(groups)], axis=1)
    all_ids = jnp.concatenate([info_in[h, 1:2, :] for h in range(groups)], axis=1)
    owner = jnp.concatenate([jnp.full((1, count), h, F32) for h in range(groups)], axis=1)
    share = share_rows * LANES
    local = all_rows - (group * share).astype(F32)
    mine = jnp.logical_and(local >= 0.0, local < share)
    line = jnp.floor(local * (1.0 / LANES))
    met_high = jnp.where(mine, owner * share_rows + line, -1.0)
    met_low = local - line * LANES

    def numbered(size):
        return iota((size, groups * count), 0).astype(F32)

    met_hot = jnp.where(numbered(LANES) == met_low, 1.0, 0.0).astype(BF16)
    met_values = fast_dot(inverse_acc[...].astype(BF16), met_hot)
    met_here = numbered(row_blocks) == met_high
    met_row = jnp.sum(
        jnp.where(met_here, met_values[0:row_blocks], 0.0), axis=0, keepdims=True
    )
    met_lane = jnp.sum(
        jnp.where(met_here, met_values[row_blocks : 2 * row_blocks], 0.0), axis=0, keepdims=True
    )
    meet_rows[...] = jnp.where(
        numbered(mult_rows) == jnp.abs(met_row) - 1.0, jnp.where(met_row > 0.0, 1.0, -1.0), 0.0
    )
    meet_lanes[...] = jnp.where(numbered(LANES) == met_lane, 1.0, 0.0)
    coarse_count = inverse_hbm.shape[0]
    hot_meets[...] = jnp.where(numbered(coarse_count) == all_ids, 1.0, 0.0)
    finish(copies_c)

    for p in range(patches):
        total = out_in[p * dup]
        for u in range(1, dup):
            total = total + out_in[p * dup + u]
        top, rest_part = halves(total)
        table[p * chunk : (p + 1) * chunk, 0:slots] = top
        table[p * chunk : (p + 1) * chunk, slots : 2 * slots] = rest_part
    lookup = table[...].astype(BF16)
    places = iota((table_rows, LANES), 0).astype(F32)

    def pick_step(offset, carry):
        peer = group_peer(offset)
        pick_for(peer)
        group_copy(picked.at[peer], owner_in, e_send, e_recv, offset, peer).start()
        return carry

    def pick_for(h):
        rows, columns = row_of[h], slot_of[h]
        found = []
        for i in range(0, share_rows, 2):
            hot = jnp.concatenate(
                [
                    one_hot(slot_numbers, columns[i : i + 1]),
                    one_hot(slot_numbers, columns[i + 1 : i + 2]),
                ],
                axis=1,
            )
            both = fast_dot(lookup, jnp.concatenate([hot, hot], axis=0))
            for u in range(2):
                here = places == rows[i + u : i + u + 1]
                found.append(
                    jnp.sum(
                        jnp.where(here, both[:, u * LANES : (u + 1) * LANES], 0.0),
                        axis=0,
                        keepdims=True,
                    )
                )
        picked[h] = jnp.concatenate(found, axis=0)

    lax.fori_loop(1, groups, pick_step, 0)
    pick_for(group)

    owner_in[group] = picked[group]
    prim_high = lax.shift_right_logical(primal, 7)
    prim_low = jnp.bitwise_and(primal, LANES - 1)
    hot_high = jnp.where(iota((row_blocks, count), 0) == prim_high, 1.0, 0.0)
    hot_low = jnp.where(iota((LANES, count), 0) == prim_low, 1.0, 0.0)
    hot_coarse = jnp.where(iota((coarse_count, count), 0) == coarse_ids, 1.0, 0.0)
    flat = jnp.concatenate([picked[h] for h in range(groups)], axis=0)
    primal_values = jnp.sum(hot_dot(flat, hot_low) * hot_high, axis=0, keepdims=True)
    coarse_send[...] = hot_dot(jnp.broadcast_to(primal_values, (8, count)), hot_coarse, NT)[0:1]
    copies_d = send_all(coarse_send, coarse_in, d_send, d_recv)
    finish(
        [
            group_copy(
                picked.at[group_peer(offset)], owner_in, e_send, e_recv, offset, group_peer(offset)
            )
            for offset in range(1, groups)
        ]
    )

    owners = jnp.concatenate([owner_in[h] for h in range(groups)], axis=0)
    top, rest_part = halves(owners)
    owner_table = jnp.concatenate([top, rest_part], axis=1).astype(BF16)

    def image_step(block, carry):
        base = pl.multiple_of(block * 8, 8)
        lane_base = pl.multiple_of(block * 8 * LANES, 8 * LANES)
        pairs = pair_ref[:, pl.ds(lane_base, 8 * LANES)]
        high = lax.shift_right_logical(pairs, 7)
        low = jnp.bitwise_and(pairs, LANES - 1).astype(F32)
        found = []
        for i in range(8):
            lanes = slice(i * LANES, (i + 1) * LANES)
            hot = jnp.concatenate(
                [one_hot(lane_numbers, low[0:1, lanes]), one_hot(lane_numbers, low[1:2, lanes])],
                axis=1,
            )
            both = fast_dot(owner_table, jnp.concatenate([hot, hot], axis=0))
            place = iota((row_blocks, LANES), 0)
            jump = jnp.where(place == high[0:1, lanes], both[:, 0:LANES], 0.0) - jnp.where(
                place == high[1:2, lanes], both[:, LANES : 2 * LANES], 0.0
            )
            found.append(jnp.sum(jump, axis=0, keepdims=True))
        image[pl.ds(base, 8), :] = jnp.concatenate(found, axis=0)
        return carry

    lax.fori_loop(0, mult_rows // 8, image_step, 0)

    inputs["inverse"].wait()
    finish(copies_d)
    coarse = sum(coarse_in[d] for d in range(groups * pencils))
    lifted = split_dot(jnp.broadcast_to(coarse, (8, coarse_count)), inverse_ref[...], NT)
    lifts = hot_dot(lifted, hot_meets[...])[0:1]
    jump_lift = hot_dot(meet_rows[...] * lifts, meet_lanes[...], NT)

    for name in ("resid", "scale"):
        inputs[name].wait()
    resid, search, scale, jumps = resid_ref[...], dir_ref[...], scale_ref[...], image[...] + jump_lift
    scaled_resid, scaled_jump = scale * resid, scale * jumps

    def total_of(values):
        return jnp.sum(jnp.sum(values, axis=0, keepdims=True), axis=1, keepdims=True)

    parts = [
        total_of(resid * scaled_resid),
        total_of(search * jumps),
        total_of(scaled_resid * jumps),
        total_of(scaled_jump * jumps),
    ]
    lane = iota((1, LANES), 1)
    sums_send[...] = sum(jnp.where(lane == n, value, 0.0) for n, value in enumerate(parts))
    finish(send_all(sums_send, sums_in, f_send, f_recv))
    sums = sum(sums_in[d] for d in range(groups * pencils))
    totals = [sums[:, n : n + 1] for n in range(4)]
    old, curvature = totals[0], totals[1]
    alpha = old / curvature
    new = old - 2.0 * alpha * totals[2] + alpha * (alpha * totals[3])
    image_out[...] = jumps
    alpha_out[...] = jnp.broadcast_to(alpha, alpha_out.shape)
    beta_out[...] = jnp.broadcast_to(new / old, beta_out.shape)


def body(
    groups,
    pencils,
    mult_iterate,
    residual,
    direction,
    mult_scale,
    eigen_basis,
    eigen_values,
    elastic_coef,
    coarse_inverse,
    send_pos,
    pair_slots,
    prim_rows,
    coarse_idx,
):
    mult_rows = direction.shape[-1] // LANES
    rows_count = send_pos.shape[-1]
    row_blocks = rows_count // LANES
    share_rows = row_blocks // groups
    patches, _, extent, _ = eigen_basis.shape
    comps = elastic_coef.shape[1]
    pairs = pair_slots.reshape(pair_slots.shape[2:])
    primal, coarse_ids = prim_rows.reshape(1, -1), coarse_idx.reshape(1, -1)
    slab = extent // pencils
    slots = 4 * extent
    width = comps * extent // (pencils // patches)
    chunk = slab * comps
    table_rows = patches * chunk
    coarse_count = coarse_inverse.shape[0]
    primal_count = primal.shape[1]
    devices = groups * pencils

    def vmem(*shape):
        return pltpu.VMEM(shape, F32)

    def index(*shape):
        return pltpu.VMEM(shape, jnp.int32)

    shape = (mult_rows, LANES)
    share = (groups, share_rows, LANES)
    pencil_sems = pltpu.SemaphoreType.DMA((pencils,))
    device_sems = pltpu.SemaphoreType.DMA((devices,))
    group_sems = pltpu.SemaphoreType.DMA((groups,))
    scratch = [
        vmem(2 * row_blocks, LANES),
        vmem(*share),
        vmem(*share),
        vmem(*share),
        vmem(*share),
        vmem(2 * table_rows, slots),
        vmem(patches, chunk, slots),
        vmem(pencils, chunk, slots),
        vmem(slots, slots),
        vmem(slots, slots),
        vmem(comps * extent, width),
        vmem(slots, width),
        vmem(extent, width),
        vmem(extent, width),
        vmem(extent, width),
        vmem(slots, width),
        vmem(pencils, chunk, slots),
        vmem(pencils, chunk, slots),
        vmem(table_rows, 2 * slots),
        vmem(*share),
        vmem(1, coarse_count),
        vmem(devices, 1, coarse_count),
        vmem(*share),
        vmem(mult_rows, LANES),
        vmem(1, LANES),
        vmem(devices, 1, LANES),
        vmem(8, primal_count),
        vmem(groups, 8, primal_count),
        vmem(2 * row_blocks, LANES),
        vmem(coarse_count, groups * primal_count),
        vmem(mult_rows, groups * primal_count),
        vmem(LANES, groups * primal_count),
        group_sems,
        group_sems,
        pencil_sems,
        pencil_sems,
        pencil_sems,
        pencil_sems,
        device_sems,
        device_sems,
        group_sems,
        group_sems,
        group_sems,
        group_sems,
        device_sems,
        device_sems,
        vmem(*shape),
        vmem(*shape),
        vmem(*shape),
        vmem(*eigen_basis.shape[1:]),
        vmem(3, patches, extent),
        vmem(comps, patches, 3),
        vmem(coarse_count, coarse_count),
        index(*share),
        index(*pairs.shape),
        index(*primal.shape),
        index(*coarse_ids.shape),
        vmem(extent, width),
        vmem(extent, width),
        vmem(extent, width),
        pltpu.SemaphoreType.DMA((11,)),
    ]
    image, alpha, beta = pl.pallas_call(
        functools.partial(kernel, groups, pencils),
        out_shape=[jax.ShapeDtypeStruct(shape, F32)] * 3,
        in_specs=[pl.BlockSpec(memory_space=pltpu.HBM)] * 11,
        out_specs=[pl.BlockSpec(memory_space=pltpu.VMEM)] * 3,
        scratch_shapes=scratch,
        compiler_params=pltpu.CompilerParams(
            collective_id=0, has_side_effects=True, vmem_limit_bytes=64 * 1024 * 1024 - 65536
        ),
        name="tearing_step",
    )(
        residual.reshape(shape),
        direction.reshape(shape),
        mult_scale.reshape(shape),
        eigen_basis,
        eigen_values.transpose(1, 0, 2),
        elastic_coef.transpose(1, 0, 2),
        coarse_inverse,
        send_pos.reshape(share),
        pairs,
        primal,
        coarse_ids,
    )
    full = mult_iterate.shape
    image, alpha, beta = image.reshape(full), alpha.reshape(full), beta.reshape(full)
    next_resid = residual - alpha * image
    next_dir = mult_scale * next_resid + beta * direction
    return mult_iterate + alpha * direction, next_resid, next_dir


def solution(mesh):
    rows = P("group", "pencil", None)
    in_specs = (
        rows,
        rows,
        rows,
        rows,
        P("group", None, None, None),
        P("group", None, None),
        P("group", None, None),
        P(),
        rows,
        P("group", "pencil", None, None),
        rows,
        rows,
    )
    return jax.shard_map(
        functools.partial(body, mesh.shape["group"], mesh.shape["pencil"]),
        mesh=mesh,
        in_specs=in_specs,
        out_specs=(rows, rows, rows),
        check_vma=False,
    )
```

```python
import functools

import jax
import jax.numpy as jnp
from jax import lax
from jax.experimental import pallas as pl
from jax.experimental.pallas import tpu as pltpu
from jax.sharding import PartitionSpec as P

LANES = 128
F32 = jnp.float32
BF16 = jnp.bfloat16
MESH = pl.DeviceIdType.MESH
NT = (((1,), (1,)), ((), ()))
NN = (((1,), (0,)), ((), ()))


def fast_dot(left, right, dims=NN):
    return lax.dot_general(left, right, dims, preferred_element_type=F32)


def halves(values):
    top = values.astype(BF16).astype(F32)
    return top, values - top


def split_dot(left, right, dims=NN):
    left_top, left_rest = (half.astype(BF16) for half in halves(left))
    right_top, right_rest = (half.astype(BF16) for half in halves(right))
    return (
        fast_dot(left_top, right_top, dims)
        + fast_dot(left_top, right_rest, dims)
        + fast_dot(left_rest, right_top, dims)
    )


def hot_dot(left, right, dims=NN):
    top, rest = (half.astype(BF16) for half in halves(left))
    hot = right.astype(BF16)
    return fast_dot(top, hot, dims) + fast_dot(rest, hot, dims)


def floor_div(values, divisor):
    return ((values.astype(F32) + 0.5) * (1.0 / divisor)).astype(jnp.int32)


def iota(shape, dim):
    return lax.broadcasted_iota(jnp.int32, shape, dim)


def column(row):
    size = row.shape[1]
    diagonal = iota((size, size), 0) == iota((size, size), 1)
    return jnp.sum(jnp.where(diagonal, row, 0.0), axis=1, keepdims=True)


def numbers(count):
    return iota((count, LANES), 0).astype(F32).astype(BF16).reshape(count // 16, 16, LANES)


def packed(row):
    return jnp.broadcast_to(row, (16, LANES)).astype(BF16)[None]


def placed(counts, row, *values):
    here = counts == packed(row)
    size = counts.shape[0] * 16
    zero = jnp.zeros((), BF16)
    return [jnp.where(here, packed(value), zero).reshape(size, LANES) for value in values]


def one_hot(counts, row):
    here = counts == packed(row)
    return jnp.where(here, jnp.ones((), BF16), jnp.zeros((), BF16)).reshape(-1, LANES)


def block_diagonal(blocks):
    total = sum(block.shape[1] for block in blocks)
    rows, before = [], 0
    for block in blocks:
        height, width = block.shape
        parts = [block]
        if before:
            parts = [jnp.zeros((height, before), F32)] + parts
        if total - before - width:
            parts = parts + [jnp.zeros((height, total - before - width), F32)]
        rows.append(jnp.concatenate(parts, axis=1) if len(parts) > 1 else block)
        before += width
    return jnp.concatenate(rows, axis=0)


def kernel(
    groups,
    pencils,
    resid_hbm,
    dir_hbm,
    scale_hbm,
    basis_hbm,
    values_hbm,
    coef_hbm,
    inverse_hbm,
    pos_hbm,
    pair_hbm,
    prim_hbm,
    cidx_hbm,
    image_out,
    alpha_out,
    beta_out,
    back_acc,
    back_send,
    rows_in,
    row_of,
    slot_of,
    load_acc,
    load_send,
    load_in,
    diag_t,
    diag,
    diag_x,
    fwd,
    y_first,
    y_last,
    y_weight,
    bwd,
    out_send,
    out_in,
    table,
    picked,
    coarse_send,
    coarse_in,
    owner_in,
    image,
    sums_send,
    sums_in,
    info_send,
    info_in,
    inverse_acc,
    hot_meets,
    meet_rows,
    meet_lanes,
    a_send,
    a_recv,
    b_send,
    b_recv,
    c_send,
    c_recv,
    d_send,
    d_recv,
    i_send,
    i_recv,
    e_send,
    e_recv,
    f_send,
    f_recv,
    resid_ref,
    dir_ref,
    scale_ref,
    basis_ref,
    values_ref,
    coef_ref,
    inverse_ref,
    pos_ref,
    pair_ref,
    prim_ref,
    cidx_ref,
    xz_weight,
    z_first,
    z_last,
    input_sem,
):
    group = lax.axis_index("group")
    pencil = lax.axis_index("pencil")
    patches, _, extent, _ = basis_hbm.shape
    comps = coef_hbm.shape[0]
    slab = extent // pencils
    share_rows = pos_ref.shape[1]
    row_blocks = groups * share_rows
    mult_rows = dir_ref.shape[0]
    slots = 4 * extent
    dup = pencils // patches
    local_i = extent // dup
    width = comps * local_i
    chunk = slab * comps
    table_rows = patches * chunk
    patch = pencil // dup
    part = lax.rem(pencil, dup)
    device = group * pencils + pencil

    def group_peer(offset):
        return lax.rem(group + offset, groups)

    def pencil_peer(offset):
        return lax.rem(pencil + offset, pencils)

    def group_copy(src, landing, send, recv, offset, peer):
        return pltpu.make_async_remote_copy(
            src_ref=src,
            dst_ref=landing.at[group],
            send_sem=send.at[offset],
            recv_sem=recv.at[offset],
            device_id=(peer, pencil),
            device_id_type=MESH,
        )

    def send_group(src_of, landing, send, recv):
        copies = []
        for offset in range(1, groups):
            peer = group_peer(offset)
            copy = group_copy(src_of(peer), landing, send, recv, offset, peer)
            copy.start()
            copies.append(copy)
        return copies

    def send_pencil(src_of, landing, send, recv):
        copies = []
        for offset in range(1, pencils):
            peer = pencil_peer(offset)
            copy = pltpu.make_async_remote_copy(
                src_ref=src_of(peer),
                dst_ref=landing.at[pencil],
                send_sem=send.at[offset],
                recv_sem=recv.at[offset],
                device_id=(group, peer),
                device_id_type=MESH,
            )
            copy.start()
            copies.append(copy)
        return copies

    def device_peer(number):
        return group_peer(number // pencils), pencil_peer(lax.rem(number, pencils))

    def all_copy(src, landing, send, recv, number):
        return pltpu.make_async_remote_copy(
            src_ref=src,
            dst_ref=landing.at[device],
            send_sem=send.at[number],
            recv_sem=recv.at[number],
            device_id=device_peer(number),
            device_id_type=MESH,
        )

    def each_device(action):
        def step(number, carry):
            action(number)
            return carry

        lax.fori_loop(1, groups * pencils, step, 0)

    def send_all(src, landing, send, recv):
        each_device(lambda number: all_copy(src, landing, send, recv, number).start())
        landing[device] = src[...]

    def finish_all(src, landing, send, recv):
        each_device(lambda number: all_copy(src, landing, send, recv, number).wait())

    def finish(copies):
        for copy in copies:
            copy.wait_recv()
        for copy in copies:
            copy.wait_send()

    barrier = pltpu.get_barrier_semaphore()
    each_device(
        lambda number: pl.semaphore_signal(
            barrier, inc=1, device_id=device_peer(number), device_id_type=MESH
        )
    )

    inputs = {}
    for number, (name, source, target) in enumerate(
        [
            ("dir", dir_hbm, dir_ref),
            ("pair", pair_hbm, pair_ref),
            ("pos", pos_hbm, pos_ref),
            ("basis", basis_hbm.at[patch], basis_ref),
            ("values", values_hbm, values_ref),
            ("coef", coef_hbm, coef_ref),
            ("prim", prim_hbm, prim_ref),
            ("cidx", cidx_hbm, cidx_ref),
            ("inverse", inverse_hbm, inverse_ref),
            ("resid", resid_hbm, resid_ref),
            ("scale", scale_hbm, scale_ref),
        ]
    ):
        inputs[name] = pltpu.make_async_copy(source, target, input_sem.at[number])
        inputs[name].start()

    back_acc[...] = jnp.zeros_like(back_acc)
    row_numbers = numbers(row_blocks)
    lane_numbers = numbers(LANES)
    slot_numbers = numbers(slots)
    table_numbers = numbers(table_rows)
    inputs["dir"].wait()
    inputs["pair"].wait()

    def back_step(block, carry):
        base = pl.multiple_of(block * 8, 8)
        lane_base = pl.multiple_of(block * 8 * LANES, 8 * LANES)
        values = dir_ref[pl.ds(base, 8), :]
        pairs = pair_ref[:, pl.ds(lane_base, 8 * LANES)]
        high = lax.shift_right_logical(pairs, 7).astype(F32)
        low = jnp.bitwise_and(pairs, LANES - 1).astype(F32)
        tops, rests = halves(values)
        left, right = [], []
        for i in range(8):
            lanes = slice(i * LANES, (i + 1) * LANES)
            for side, sign in ((0, 1.0), (1, -1.0)):
                left.append(
                    jnp.concatenate(
                        placed(
                            row_numbers,
                            high[side : side + 1, lanes],
                            sign * tops[i : i + 1],
                            sign * rests[i : i + 1],
                        ),
                        axis=0,
                    )
                )
                right.append(one_hot(lane_numbers, low[side : side + 1, lanes]))
        back_acc[...] += fast_dot(
            jnp.concatenate(left, axis=1), jnp.concatenate(right, axis=1), NT
        )
        return carry

    lax.fori_loop(0, mult_rows // 8, back_step, 0)
    for h in range(groups):
        rows = slice(h * share_rows, (h + 1) * share_rows)
        low_rows = slice(row_blocks + h * share_rows, row_blocks + (h + 1) * share_rows)
        back_send[h] = back_acc[rows, :] + back_acc[low_rows, :]

    pl.semaphore_wait(barrier, groups * pencils - 1)
    copies_a = send_group(lambda peer: back_send.at[peer], rows_in, a_send, a_recv)
    rows_in[group] = back_send[group]

    for name in ("prim", "cidx"):
        inputs[name].wait()
    primal, coarse_ids = prim_ref[...], cidx_ref[...]
    count = primal.shape[1]
    info_send[...] = jnp.concatenate(
        [primal.astype(F32), coarse_ids.astype(F32), jnp.zeros((6, count), F32)], axis=0
    )
    copies_i = send_group(lambda peer: info_send, info_in, i_send, i_recv)
    info_in[group] = info_send[...]

    inputs["pos"].wait()
    cells = pos_ref[...]
    cycle = 4 * extent - 4
    plane = floor_div(cells, cycle)
    spot = cells - plane * cycle
    slot_of[...] = (
        spot
        + jnp.where(spot >= extent, 1, 0)
        + jnp.where(spot >= 2 * extent - 2, 2, 0)
        + jnp.where(spot >= 3 * extent - 4, 1, 0)
    ).astype(F32)
    x_index = floor_div(plane, patches * comps)
    rest = plane - x_index * (patches * comps)
    p_index = floor_div(rest, comps)
    c_index = rest - p_index * comps
    row_of[...] = (p_index * chunk + c_index * slab + x_index).astype(F32)

    load_acc[...] = jnp.zeros_like(load_acc)


    def load_step(offset, carry):
        h = lax.rem(group - offset + groups, groups)

        @pl.when(offset > 0)
        def _():
            group_copy(back_send.at[h], rows_in, a_send, a_recv, offset, h).wait_recv()

        values = rows_in[h]
        rows, columns = row_of[h], slot_of[h]
        tops, rests = halves(values)
        left, right = [], []
        for i in range(share_rows):
            left.append(
                jnp.concatenate(
                    placed(
                        table_numbers, rows[i : i + 1], tops[i : i + 1], rests[i : i + 1]
                    ),
                    axis=0,
                )
            )
            right.append(one_hot(slot_numbers, columns[i : i + 1]))
        load_acc[...] += fast_dot(
            jnp.concatenate(left, axis=1), jnp.concatenate(right, axis=1), NT
        )
        return carry

    lax.fori_loop(0, groups, load_step, 0)
    for copy in copies_a:
        copy.wait_send()
    for p in range(patches):
        load_send[p] = (
            load_acc[p * chunk : (p + 1) * chunk, :]
            + load_acc[table_rows + p * chunk : table_rows + (p + 1) * chunk, :]
        )
    copies_b = send_pencil(lambda peer: load_send.at[peer // dup], load_in, b_send, b_recv)
    load_in[pencil] = load_send[patch]

    for name in ("basis", "values", "coef"):
        inputs[name].wait()
    basis_x = basis_ref[0]
    basis_y = basis_ref[1]
    basis_z = basis_ref[2]

    def of_patch(ref, row):
        return sum(jnp.where(patch == p, ref[row, p : p + 1, :], 0.0) for p in range(patches))

    spectrum = [of_patch(values_ref, axis) for axis in range(3)]
    coef = [of_patch(coef_ref, c) for c in range(comps)]
    along_x = spectrum[0]
    if dup > 1:
        basis_x = sum(
            jnp.where(part == u, basis_x[:, u * local_i : (u + 1) * local_i], 0.0)
            for u in range(dup)
        )
        along_x = sum(
            jnp.where(part == u, along_x[:, u * local_i : (u + 1) * local_i], 0.0)
            for u in range(dup)
        )
    diag[...] = block_diagonal([basis_z, basis_y, basis_y, basis_z])
    basis_yt, basis_zt = basis_y.T, basis_z.T
    diag_t[...] = block_diagonal([basis_zt, basis_yt, basis_yt, basis_zt])
    diag_x[...] = block_diagonal([basis_x] * comps)
    ones = jnp.ones((1, local_i), F32)
    weight_x = jnp.concatenate([coef[c][:, 0:1] * along_x for c in range(comps)], axis=1)
    weight_y = jnp.concatenate([coef[c][:, 1:2] * ones for c in range(comps)], axis=1)
    weight_z = jnp.concatenate([coef[c][:, 2:3] * ones for c in range(comps)], axis=1)
    y_weight[...] = column(spectrum[1]) * weight_y
    wide = jnp.ones((1, width), F32)
    y_first[...] = column(basis_y[0:1]) * wide
    y_last[...] = column(basis_y[extent - 1 : extent]) * wide
    xz_weight[...] = weight_x + column(spectrum[2]) * weight_z
    z_first[...] = column(basis_z[0:1]) * wide
    z_last[...] = column(basis_z[extent - 1 : extent]) * wide
    bwd[...] = jnp.zeros_like(bwd)
    inverse_acc[...] = jnp.zeros_like(inverse_acc)
    lane_of = iota((1, LANES), 1).astype(F32)

    def inverse_step(block, carry):
        lane_base = pl.multiple_of(block * 8 * LANES, 8 * LANES)
        pairs = pair_ref[:, pl.ds(lane_base, 8 * LANES)]
        high = lax.shift_right_logical(pairs, 7).astype(F32)
        low = jnp.bitwise_and(pairs, LANES - 1).astype(F32)
        first = jnp.zeros((1, LANES), F32) + (block * 8 + 1).astype(F32)
        left, right = [], []
        for i in range(8):
            lanes = slice(i * LANES, (i + 1) * LANES)
            for side, sign in ((0, 1.0), (1, -1.0)):
                left.append(
                    jnp.concatenate(
                        placed(
                            row_numbers, high[side : side + 1, lanes], sign * (first + i), lane_of
                        ),
                        axis=0,
                    )
                )
                right.append(one_hot(lane_numbers, low[side : side + 1, lanes]))
        inverse_acc[...] += fast_dot(
            jnp.concatenate(left, axis=1), jnp.concatenate(right, axis=1), NT
        )
        return carry

    lax.fori_loop(0, mult_rows // 8, inverse_step, 0)
    finish(copies_b)

    sides = jnp.concatenate(
        [load_in[s, c * slab : (c + 1) * slab, :] for c in range(comps) for s in range(pencils)],
        axis=0,
    )
    fwd[...] = split_dot(split_dot(diag_t[...], sides, NT), diag_x[...])

    def solve_step(block, carry):
        base = pl.multiple_of(block * 8, 8)
        first = y_first[pl.ds(base, 8), :]
        last = y_last[pl.ds(base, 8), :]
        weight = y_weight[pl.ds(base, 8), :]
        side_b = fwd[pl.ds(extent + base, 8), :]
        side_c = fwd[pl.ds(2 * extent + base, 8), :]
        out_b, out_c = [], []
        for i in range(8):
            row = slice(i, i + 1)
            row_first = jnp.broadcast_to(first[row], (8, width))
            row_last = jnp.broadcast_to(last[row], (8, width))
            row_weight = jnp.broadcast_to(weight[row], (8, width))
            row_b = jnp.broadcast_to(side_b[row], (8, width))
            row_c = jnp.broadcast_to(side_c[row], (8, width))
            sum_b = sum_c = jnp.zeros((8, width), F32)
            for k in range(0, extent, 8):
                here = slice(k, k + 8)
                there = slice(3 * extent + k, 3 * extent + k + 8)
                z_one, z_two = z_first[here, :], z_last[here, :]
                spectral = (
                    row_first * fwd[here, :]
                    + row_last * fwd[there, :]
                    + row_b * z_one
                    + row_c * z_two
                )
                weights = xz_weight[here, :] + row_weight
                guess = pl.reciprocal(weights, approx=True)
                scaled = spectral * (guess * (2.0 - weights * guess))
                bwd[here, :] += row_first * scaled
                bwd[there, :] += row_last * scaled
                sum_b = sum_b + z_one * scaled
                sum_c = sum_c + z_two * scaled
            out_b.append(sum_b)
            out_c.append(sum_c)
        for start, parts in ((extent, out_b), (2 * extent, out_c)):
            bwd[pl.ds(start + base, 8), :] = jnp.concatenate(
                [jnp.sum(part, axis=0, keepdims=True) for part in parts], axis=0
            )
        return carry

    lax.fori_loop(0, extent // 8, solve_step, 0)
    cells_out = split_dot(diag_x[...], split_dot(diag[...], bwd[...]), NT)
    for s in range(pencils):
        out_send[s] = jnp.concatenate(
            [
                cells_out[c * extent + s * slab : c * extent + (s + 1) * slab, :]
                for c in range(comps)
            ],
            axis=0,
        )
    copies_c = send_pencil(lambda peer: out_send.at[peer], out_in, c_send, c_recv)
    out_in[pencil] = out_send[pencil]
    finish(copies_i)
    all_rows = jnp.concatenate([info_in[h, 0:1, :] for h in range(groups)], axis=1)
    all_ids = jnp.concatenate([info_in[h, 1:2, :] for h in range(groups)], axis=1)
    owner = jnp.concatenate([jnp.full((1, count), h, F32) for h in range(groups)], axis=1)
    share = share_rows * LANES
    local = all_rows - (group * share).astype(F32)
    mine = jnp.logical_and(local >= 0.0, local < share)
    line = jnp.floor(local * (1.0 / LANES))
    met_high = jnp.where(mine, owner * share_rows + line, -1.0)
    met_low = local - line * LANES

    def numbered(size):
        return iota((size, groups * count), 0).astype(F32)

    met_hot = jnp.where(numbered(LANES) == met_low, 1.0, 0.0).astype(BF16)
    met_values = fast_dot(inverse_acc[...].astype(BF16), met_hot)
    met_here = numbered(row_blocks) == met_high
    met_row = jnp.sum(
        jnp.where(met_here, met_values[0:row_blocks], 0.0), axis=0, keepdims=True
    )
    met_lane = jnp.sum(
        jnp.where(met_here, met_values[row_blocks : 2 * row_blocks], 0.0), axis=0, keepdims=True
    )
    meet_rows[...] = jnp.where(
        numbered(mult_rows) == jnp.abs(met_row) - 1.0, jnp.where(met_row > 0.0, 1.0, -1.0), 0.0
    )
    meet_lanes[...] = jnp.where(numbered(LANES) == met_lane, 1.0, 0.0)
    coarse_count = inverse_hbm.shape[0]
    hot_meets[...] = jnp.where(numbered(coarse_count) == all_ids, 1.0, 0.0)
    finish(copies_c)

    for p in range(patches):
        total = out_in[p * dup]
        for u in range(1, dup):
            total = total + out_in[p * dup + u]
        top, rest_part = halves(total)
        table[p * chunk : (p + 1) * chunk, 0:slots] = top
        table[p * chunk : (p + 1) * chunk, slots : 2 * slots] = rest_part
    lookup = table[...].astype(BF16)
    places = iota((table_rows, LANES), 0).astype(F32)

    def pick_step(offset, carry):
        h = group_peer(offset)
        rows, columns = row_of[h], slot_of[h]
        found = []
        for i in range(0, share_rows, 2):
            hot = jnp.concatenate(
                [
                    one_hot(slot_numbers, columns[i : i + 1]),
                    one_hot(slot_numbers, columns[i + 1 : i + 2]),
                ],
                axis=1,
            )
            both = fast_dot(lookup, jnp.concatenate([hot, hot], axis=0))
            for u in range(2):
                here = places == rows[i + u : i + u + 1]
                found.append(
                    jnp.sum(
                        jnp.where(here, both[:, u * LANES : (u + 1) * LANES], 0.0),
                        axis=0,
                        keepdims=True,
                    )
                )
        picked[h] = jnp.concatenate(found, axis=0)

        @pl.when(offset < groups)
        def _():
            group_copy(picked.at[h], owner_in, e_send, e_recv, offset, h).start()

        return carry

    lax.fori_loop(1, groups + 1, pick_step, 0)

    owner_in[group] = picked[group]
    prim_high = lax.shift_right_logical(primal, 7)
    prim_low = jnp.bitwise_and(primal, LANES - 1)
    hot_high = jnp.where(iota((row_blocks, count), 0) == prim_high, 1.0, 0.0)
    hot_low = jnp.where(iota((LANES, count), 0) == prim_low, 1.0, 0.0)
    hot_coarse = jnp.where(iota((coarse_count, count), 0) == coarse_ids, 1.0, 0.0)
    flat = jnp.concatenate([picked[h] for h in range(groups)], axis=0)
    primal_values = jnp.sum(hot_dot(flat, hot_low) * hot_high, axis=0, keepdims=True)
    coarse_send[...] = hot_dot(jnp.broadcast_to(primal_values, (8, count)), hot_coarse, NT)[0:1]
    send_all(coarse_send, coarse_in, d_send, d_recv)
    finish(
        [
            group_copy(
                picked.at[group_peer(offset)], owner_in, e_send, e_recv, offset, group_peer(offset)
            )
            for offset in range(1, groups)
        ]
    )

    owners = jnp.concatenate([owner_in[h] for h in range(groups)], axis=0)
    top, rest_part = halves(owners)
    owner_table = jnp.concatenate([top, rest_part], axis=1).astype(BF16)

    def image_step(block, carry):
        base = pl.multiple_of(block * 8, 8)
        lane_base = pl.multiple_of(block * 8 * LANES, 8 * LANES)
        pairs = pair_ref[:, pl.ds(lane_base, 8 * LANES)]
        high = lax.shift_right_logical(pairs, 7)
        low = jnp.bitwise_and(pairs, LANES - 1).astype(F32)
        found = []
        for i in range(8):
            lanes = slice(i * LANES, (i + 1) * LANES)
            hot = jnp.concatenate(
                [one_hot(lane_numbers, low[0:1, lanes]), one_hot(lane_numbers, low[1:2, lanes])],
                axis=1,
            )
            both = fast_dot(owner_table, jnp.concatenate([hot, hot], axis=0))
            place = iota((row_blocks, LANES), 0)
            jump = jnp.where(place == high[0:1, lanes], both[:, 0:LANES], 0.0) - jnp.where(
                place == high[1:2, lanes], both[:, LANES : 2 * LANES], 0.0
            )
            found.append(jnp.sum(jump, axis=0, keepdims=True))
        image[pl.ds(base, 8), :] = jnp.concatenate(found, axis=0)
        return carry

    lax.fori_loop(0, mult_rows // 8, image_step, 0)

    inputs["inverse"].wait()
    finish_all(coarse_send, coarse_in, d_send, d_recv)
    coarse = jnp.sum(coarse_in[...], axis=0)
    lifted = split_dot(jnp.broadcast_to(coarse, (8, coarse_count)), inverse_ref[...], NT)
    lifts = hot_dot(lifted, hot_meets[...])[0:1]
    jump_lift = hot_dot(meet_rows[...] * lifts, meet_lanes[...], NT)

    for name in ("resid", "scale"):
        inputs[name].wait()
    resid, search, scale, jumps = resid_ref[...], dir_ref[...], scale_ref[...], image[...] + jump_lift
    scaled_resid, scaled_jump = scale * resid, scale * jumps

    def total_of(values):
        return jnp.sum(jnp.sum(values, axis=0, keepdims=True), axis=1, keepdims=True)

    parts = [
        total_of(resid * scaled_resid),
        total_of(search * jumps),
        total_of(scaled_resid * jumps),
        total_of(scaled_jump * jumps),
    ]
    lane = iota((1, LANES), 1)
    sums_send[...] = sum(jnp.where(lane == n, value, 0.0) for n, value in enumerate(parts))
    send_all(sums_send, sums_in, f_send, f_recv)
    finish_all(sums_send, sums_in, f_send, f_recv)
    sums = jnp.sum(sums_in[...], axis=0)
    totals = [sums[:, n : n + 1] for n in range(4)]
    old, curvature = totals[0], totals[1]
    alpha = old / curvature
    new = old - 2.0 * alpha * totals[2] + alpha * (alpha * totals[3])
    image_out[...] = jumps
    alpha_out[...] = jnp.broadcast_to(alpha, alpha_out.shape)
    beta_out[...] = jnp.broadcast_to(new / old, beta_out.shape)


def body(
    groups,
    pencils,
    mult_iterate,
    residual,
    direction,
    mult_scale,
    eigen_basis,
    eigen_values,
    elastic_coef,
    coarse_inverse,
    send_pos,
    pair_slots,
    prim_rows,
    coarse_idx,
):
    mult_rows = direction.shape[-1] // LANES
    rows_count = send_pos.shape[-1]
    row_blocks = rows_count // LANES
    share_rows = row_blocks // groups
    patches, _, extent, _ = eigen_basis.shape
    comps = elastic_coef.shape[1]
    pairs = pair_slots.reshape(pair_slots.shape[2:])
    primal, coarse_ids = prim_rows.reshape(1, -1), coarse_idx.reshape(1, -1)
    slab = extent // pencils
    slots = 4 * extent
    width = comps * extent // (pencils // patches)
    chunk = slab * comps
    table_rows = patches * chunk
    coarse_count = coarse_inverse.shape[0]
    primal_count = primal.shape[1]
    devices = groups * pencils

    def vmem(*shape):
        return pltpu.VMEM(shape, F32)

    def index(*shape):
        return pltpu.VMEM(shape, jnp.int32)

    shape = (mult_rows, LANES)
    share = (groups, share_rows, LANES)
    pencil_sems = pltpu.SemaphoreType.DMA((pencils,))
    device_sems = pltpu.SemaphoreType.DMA((devices,))
    group_sems = pltpu.SemaphoreType.DMA((groups,))
    scratch = [
        vmem(2 * row_blocks, LANES),
        vmem(*share),
        vmem(*share),
        vmem(*share),
        vmem(*share),
        vmem(2 * table_rows, slots),
        vmem(patches, chunk, slots),
        vmem(pencils, chunk, slots),
        vmem(slots, slots),
        vmem(slots, slots),
        vmem(comps * extent, width),
        vmem(slots, width),
        vmem(extent, width),
        vmem(extent, width),
        vmem(extent, width),
        vmem(slots, width),
        vmem(pencils, chunk, slots),
        vmem(pencils, chunk, slots),
        vmem(table_rows, 2 * slots),
        vmem(*share),
        vmem(1, coarse_count),
        vmem(devices, 1, coarse_count),
        vmem(*share),
        vmem(mult_rows, LANES),
        vmem(1, LANES),
        vmem(devices, 1, LANES),
        vmem(8, primal_count),
        vmem(groups, 8, primal_count),
        vmem(2 * row_blocks, LANES),
        vmem(coarse_count, groups * primal_count),
        vmem(mult_rows, groups * primal_count),
        vmem(LANES, groups * primal_count),
        group_sems,
        group_sems,
        pencil_sems,
        pencil_sems,
        pencil_sems,
        pencil_sems,
        device_sems,
        device_sems,
        group_sems,
        group_sems,
        group_sems,
        group_sems,
        device_sems,
        device_sems,
        vmem(*shape),
        vmem(*shape),
        vmem(*shape),
        vmem(*eigen_basis.shape[1:]),
        vmem(3, patches, extent),
        vmem(comps, patches, 3),
        vmem(coarse_count, coarse_count),
        index(*share),
        index(*pairs.shape),
        index(*primal.shape),
        index(*coarse_ids.shape),
        vmem(extent, width),
        vmem(extent, width),
        vmem(extent, width),
        pltpu.SemaphoreType.DMA((11,)),
    ]
    image, alpha, beta = pl.pallas_call(
        functools.partial(kernel, groups, pencils),
        out_shape=[jax.ShapeDtypeStruct(shape, F32)] * 3,
        in_specs=[pl.BlockSpec(memory_space=pltpu.HBM)] * 11,
        out_specs=[pl.BlockSpec(memory_space=pltpu.VMEM)] * 3,
        scratch_shapes=scratch,
        compiler_params=pltpu.CompilerParams(
            collective_id=0, has_side_effects=True, vmem_limit_bytes=64 * 1024 * 1024 - 65536
        ),
        name="tearing_step",
    )(
        residual.reshape(shape),
        direction.reshape(shape),
        mult_scale.reshape(shape),
        eigen_basis,
        eigen_values.transpose(1, 0, 2),
        elastic_coef.transpose(1, 0, 2),
        coarse_inverse,
        send_pos.reshape(share),
        pairs,
        primal,
        coarse_ids,
    )
    full = mult_iterate.shape
    image, alpha, beta = image.reshape(full), alpha.reshape(full), beta.reshape(full)
    next_resid = residual - alpha * image
    next_dir = mult_scale * next_resid + beta * direction
    return mult_iterate + alpha * direction, next_resid, next_dir


def solution(mesh):
    rows = P("group", "pencil", None)
    in_specs = (
        rows,
        rows,
        rows,
        rows,
        P("group", None, None, None),
        P("group", None, None),
        P("group", None, None),
        P(),
        rows,
        P("group", "pencil", None, None),
        rows,
        rows,
    )
    return jax.shard_map(
        functools.partial(body, mesh.shape["group"], mesh.shape["pencil"]),
        mesh=mesh,
        in_specs=in_specs,
        out_specs=(rows, rows, rows),
        check_vma=False,
    )
```

```python
import functools

import jax
import jax.numpy as jnp
from jax import lax
from jax.experimental import pallas as pl
from jax.experimental.pallas import tpu as pltpu
from jax.sharding import PartitionSpec as P

LANES = 128
F32 = jnp.float32
BF16 = jnp.bfloat16
MESH = pl.DeviceIdType.MESH
NT = (((1,), (1,)), ((), ()))
NN = (((1,), (0,)), ((), ()))


def fast_dot(left, right, dims=NN):
    return lax.dot_general(left, right, dims, preferred_element_type=F32)


def halves(values):
    top = values.astype(BF16).astype(F32)
    return top, values - top


def split_dot(left, right, dims=NN):
    left_top, left_rest = (half.astype(BF16) for half in halves(left))
    right_top, right_rest = (half.astype(BF16) for half in halves(right))
    return (
        fast_dot(left_top, right_top, dims)
        + fast_dot(left_top, right_rest, dims)
        + fast_dot(left_rest, right_top, dims)
    )


def hot_dot(left, right, dims=NN):
    top, rest = (half.astype(BF16) for half in halves(left))
    hot = right.astype(BF16)
    return fast_dot(top, hot, dims) + fast_dot(rest, hot, dims)


def floor_div(values, divisor):
    return ((values.astype(F32) + 0.5) * (1.0 / divisor)).astype(jnp.int32)


def iota(shape, dim):
    return lax.broadcasted_iota(jnp.int32, shape, dim)


def column(row):
    size = row.shape[1]
    diagonal = iota((size, size), 0) == iota((size, size), 1)
    return jnp.sum(jnp.where(diagonal, row, 0.0), axis=1, keepdims=True)


def numbers(count):
    return iota((count, LANES), 0).astype(F32).astype(BF16).reshape(count // 16, 16, LANES)


def packed(row):
    return jnp.broadcast_to(row, (16, LANES)).astype(BF16)[None]


def placed(counts, row, *values):
    here = counts == packed(row)
    size = counts.shape[0] * 16
    zero = jnp.zeros((), BF16)
    return [jnp.where(here, packed(value), zero).reshape(size, LANES) for value in values]


def one_hot(counts, row):
    here = counts == packed(row)
    return jnp.where(here, jnp.ones((), BF16), jnp.zeros((), BF16)).reshape(-1, LANES)


def block_diagonal(blocks):
    total = sum(block.shape[1] for block in blocks)
    rows, before = [], 0
    for block in blocks:
        height, width = block.shape
        parts = [block]
        if before:
            parts = [jnp.zeros((height, before), F32)] + parts
        if total - before - width:
            parts = parts + [jnp.zeros((height, total - before - width), F32)]
        rows.append(jnp.concatenate(parts, axis=1) if len(parts) > 1 else block)
        before += width
    return jnp.concatenate(rows, axis=0)


def kernel(
    groups,
    pencils,
    resid_hbm,
    dir_hbm,
    scale_hbm,
    basis_hbm,
    values_hbm,
    coef_hbm,
    inverse_hbm,
    pos_hbm,
    pair_hbm,
    prim_hbm,
    cidx_hbm,
    image_out,
    alpha_out,
    beta_out,
    back_acc,
    back_send,
    rows_in,
    row_of,
    slot_of,
    load_acc,
    load_send,
    load_in,
    diag_t,
    diag,
    diag_x,
    fwd,
    y_first,
    y_last,
    y_weight,
    bwd,
    out_send,
    out_in,
    table,
    picked,
    coarse_send,
    coarse_in,
    owner_in,
    image,
    sums_send,
    sums_in,
    info_send,
    info_in,
    inverse_acc,
    hot_meets,
    meet_rows,
    meet_lanes,
    a_send,
    a_recv,
    b_send,
    b_recv,
    c_send,
    c_recv,
    d_send,
    d_recv,
    i_send,
    i_recv,
    e_send,
    e_recv,
    f_send,
    f_recv,
    resid_ref,
    dir_ref,
    scale_ref,
    basis_ref,
    values_ref,
    coef_ref,
    inverse_ref,
    pos_ref,
    pair_ref,
    prim_ref,
    cidx_ref,
    xz_weight,
    z_first,
    z_last,
    input_sem,
):
    group = lax.axis_index("group")
    pencil = lax.axis_index("pencil")
    patches, _, extent, _ = basis_hbm.shape
    comps = coef_hbm.shape[0]
    slab = extent // pencils
    share_rows = pos_ref.shape[1]
    row_blocks = groups * share_rows
    mult_rows = dir_ref.shape[0]
    slots = 4 * extent
    dup = pencils // patches
    local_i = extent // dup
    width = comps * local_i
    chunk = slab * comps
    table_rows = patches * chunk
    patch = pencil // dup
    part = lax.rem(pencil, dup)
    device = group * pencils + pencil

    def group_peer(offset):
        return lax.rem(group + offset, groups)

    def pencil_peer(offset):
        return lax.rem(pencil + offset, pencils)

    def group_copy(src, landing, send, recv, offset, peer):
        return pltpu.make_async_remote_copy(
            src_ref=src,
            dst_ref=landing.at[group],
            send_sem=send.at[offset],
            recv_sem=recv.at[offset],
            device_id=(peer, pencil),
            device_id_type=MESH,
        )

    def send_group(src_of, landing, send, recv):
        copies = []
        for offset in range(1, groups):
            peer = group_peer(offset)
            copy = group_copy(src_of(peer), landing, send, recv, offset, peer)
            copy.start()
            copies.append(copy)
        return copies

    def send_pencil(src_of, landing, send, recv):
        copies = []
        for offset in range(1, pencils):
            peer = pencil_peer(offset)
            copy = pltpu.make_async_remote_copy(
                src_ref=src_of(peer),
                dst_ref=landing.at[pencil],
                send_sem=send.at[offset],
                recv_sem=recv.at[offset],
                device_id=(group, peer),
                device_id_type=MESH,
            )
            copy.start()
            copies.append(copy)
        return copies

    def device_peer(number):
        return group_peer(number // pencils), pencil_peer(number % pencils)

    def all_copy(src, landing, send, recv, number):
        return pltpu.make_async_remote_copy(
            src_ref=src,
            dst_ref=landing.at[device],
            send_sem=send.at[number],
            recv_sem=recv.at[number],
            device_id=device_peer(number),
            device_id_type=MESH,
        )

    def each_device(action):
        for number in range(1, groups * pencils):
            action(number)

    def send_all(src, landing, send, recv):
        each_device(lambda number: all_copy(src, landing, send, recv, number).start())
        landing[device] = src[...]

    def finish_all(src, landing, send, recv):
        each_device(lambda number: all_copy(src, landing, send, recv, number).wait())

    def finish(copies):
        for copy in copies:
            copy.wait_recv()
        for copy in copies:
            copy.wait_send()

    barrier = pltpu.get_barrier_semaphore()
    each_device(
        lambda number: pl.semaphore_signal(
            barrier, inc=1, device_id=device_peer(number), device_id_type=MESH
        )
    )

    inputs = {}
    for number, (name, source, target) in enumerate(
        [
            ("dir", dir_hbm, dir_ref),
            ("pair", pair_hbm, pair_ref),
            ("pos", pos_hbm, pos_ref),
            ("basis", basis_hbm.at[patch], basis_ref),
            ("values", values_hbm, values_ref),
            ("coef", coef_hbm, coef_ref),
            ("prim", prim_hbm, prim_ref),
            ("cidx", cidx_hbm, cidx_ref),
            ("inverse", inverse_hbm, inverse_ref),
            ("resid", resid_hbm, resid_ref),
            ("scale", scale_hbm, scale_ref),
        ]
    ):
        inputs[name] = pltpu.make_async_copy(source, target, input_sem.at[number])
        inputs[name].start()

    back_acc[...] = jnp.zeros_like(back_acc)
    row_numbers = numbers(row_blocks)
    lane_numbers = numbers(LANES)
    slot_numbers = numbers(slots)
    table_numbers = numbers(table_rows)
    inputs["dir"].wait()
    inputs["pair"].wait()

    def back_step(block, carry):
        base = pl.multiple_of(block * 8, 8)
        lane_base = pl.multiple_of(block * 8 * LANES, 8 * LANES)
        values = dir_ref[pl.ds(base, 8), :]
        pairs = pair_ref[:, pl.ds(lane_base, 8 * LANES)]
        high = lax.shift_right_logical(pairs, 7).astype(F32)
        low = jnp.bitwise_and(pairs, LANES - 1).astype(F32)
        tops, rests = halves(values)
        left, right = [], []
        for i in range(8):
            lanes = slice(i * LANES, (i + 1) * LANES)
            for side, sign in ((0, 1.0), (1, -1.0)):
                left.append(
                    jnp.concatenate(
                        placed(
                            row_numbers,
                            high[side : side + 1, lanes],
                            sign * tops[i : i + 1],
                            sign * rests[i : i + 1],
                        ),
                        axis=0,
                    )
                )
                right.append(one_hot(lane_numbers, low[side : side + 1, lanes]))
        back_acc[...] += fast_dot(
            jnp.concatenate(left, axis=1), jnp.concatenate(right, axis=1), NT
        )
        return carry

    lax.fori_loop(0, mult_rows // 8, back_step, 0)
    for h in range(groups):
        rows = slice(h * share_rows, (h + 1) * share_rows)
        low_rows = slice(row_blocks + h * share_rows, row_blocks + (h + 1) * share_rows)
        back_send[h] = back_acc[rows, :] + back_acc[low_rows, :]

    pl.semaphore_wait(barrier, groups * pencils - 1)
    copies_a = send_group(lambda peer: back_send.at[peer], rows_in, a_send, a_recv)
    rows_in[group] = back_send[group]

    for name in ("prim", "cidx"):
        inputs[name].wait()
    primal, coarse_ids = prim_ref[...], cidx_ref[...]
    count = primal.shape[1]
    info_send[...] = jnp.concatenate(
        [primal.astype(F32), coarse_ids.astype(F32), jnp.zeros((6, count), F32)], axis=0
    )
    copies_i = send_group(lambda peer: info_send, info_in, i_send, i_recv)
    info_in[group] = info_send[...]

    inputs["pos"].wait()
    cells = pos_ref[...]
    cycle = 4 * extent - 4
    plane = floor_div(cells, cycle)
    spot = cells - plane * cycle
    slot_of[...] = (
        spot
        + jnp.where(spot >= extent, 1, 0)
        + jnp.where(spot >= 2 * extent - 2, 2, 0)
        + jnp.where(spot >= 3 * extent - 4, 1, 0)
    ).astype(F32)
    x_index = floor_div(plane, patches * comps)
    rest = plane - x_index * (patches * comps)
    p_index = floor_div(rest, comps)
    c_index = rest - p_index * comps
    row_of[...] = (p_index * chunk + c_index * slab + x_index).astype(F32)

    load_acc[...] = jnp.zeros_like(load_acc)


    def load_step(offset, carry):
        h = lax.rem(group - offset + groups, groups)

        @pl.when(offset > 0)
        def _():
            group_copy(back_send.at[h], rows_in, a_send, a_recv, offset, h).wait_recv()

        values = rows_in[h]
        rows, columns = row_of[h], slot_of[h]
        tops, rests = halves(values)
        left, right = [], []
        for i in range(share_rows):
            left.append(
                jnp.concatenate(
                    placed(
                        table_numbers, rows[i : i + 1], tops[i : i + 1], rests[i : i + 1]
                    ),
                    axis=0,
                )
            )
            right.append(one_hot(slot_numbers, columns[i : i + 1]))
        load_acc[...] += fast_dot(
            jnp.concatenate(left, axis=1), jnp.concatenate(right, axis=1), NT
        )
        return carry

    lax.fori_loop(0, groups, load_step, 0)
    for copy in copies_a:
        copy.wait_send()
    for p in range(patches):
        load_send[p] = (
            load_acc[p * chunk : (p + 1) * chunk, :]
            + load_acc[table_rows + p * chunk : table_rows + (p + 1) * chunk, :]
        )
    copies_b = send_pencil(lambda peer: load_send.at[peer // dup], load_in, b_send, b_recv)
    load_in[pencil] = load_send[patch]

    for name in ("basis", "values", "coef"):
        inputs[name].wait()
    basis_x = basis_ref[0]
    basis_y = basis_ref[1]
    basis_z = basis_ref[2]

    def of_patch(ref, row):
        return sum(jnp.where(patch == p, ref[row, p : p + 1, :], 0.0) for p in range(patches))

    spectrum = [of_patch(values_ref, axis) for axis in range(3)]
    coef = [of_patch(coef_ref, c) for c in range(comps)]
    along_x = spectrum[0]
    if dup > 1:
        basis_x = sum(
            jnp.where(part == u, basis_x[:, u * local_i : (u + 1) * local_i], 0.0)
            for u in range(dup)
        )
        along_x = sum(
            jnp.where(part == u, along_x[:, u * local_i : (u + 1) * local_i], 0.0)
            for u in range(dup)
        )
    diag[...] = block_diagonal([basis_z, basis_y, basis_y, basis_z])
    basis_yt, basis_zt = basis_y.T, basis_z.T
    diag_t[...] = block_diagonal([basis_zt, basis_yt, basis_yt, basis_zt])
    diag_x[...] = block_diagonal([basis_x] * comps)
    ones = jnp.ones((1, local_i), F32)
    weight_x = jnp.concatenate([coef[c][:, 0:1] * along_x for c in range(comps)], axis=1)
    weight_y = jnp.concatenate([coef[c][:, 1:2] * ones for c in range(comps)], axis=1)
    weight_z = jnp.concatenate([coef[c][:, 2:3] * ones for c in range(comps)], axis=1)
    y_weight[...] = column(spectrum[1]) * weight_y
    wide = jnp.ones((1, width), F32)
    y_first[...] = column(basis_y[0:1]) * wide
    y_last[...] = column(basis_y[extent - 1 : extent]) * wide
    xz_weight[...] = weight_x + column(spectrum[2]) * weight_z
    z_first[...] = column(basis_z[0:1]) * wide
    z_last[...] = column(basis_z[extent - 1 : extent]) * wide
    bwd[...] = jnp.zeros_like(bwd)
    inverse_acc[...] = jnp.zeros_like(inverse_acc)
    lane_of = iota((1, LANES), 1).astype(F32)

    def inverse_step(block, carry):
        lane_base = pl.multiple_of(block * 8 * LANES, 8 * LANES)
        pairs = pair_ref[:, pl.ds(lane_base, 8 * LANES)]
        high = lax.shift_right_logical(pairs, 7).astype(F32)
        low = jnp.bitwise_and(pairs, LANES - 1).astype(F32)
        first = jnp.zeros((1, LANES), F32) + (block * 8 + 1).astype(F32)
        left, right = [], []
        for i in range(8):
            lanes = slice(i * LANES, (i + 1) * LANES)
            for side, sign in ((0, 1.0), (1, -1.0)):
                left.append(
                    jnp.concatenate(
                        placed(
                            row_numbers, high[side : side + 1, lanes], sign * (first + i), lane_of
                        ),
                        axis=0,
                    )
                )
                right.append(one_hot(lane_numbers, low[side : side + 1, lanes]))
        inverse_acc[...] += fast_dot(
            jnp.concatenate(left, axis=1), jnp.concatenate(right, axis=1), NT
        )
        return carry

    lax.fori_loop(0, mult_rows // 8, inverse_step, 0)
    finish(copies_b)

    sides = jnp.concatenate(
        [load_in[s, c * slab : (c + 1) * slab, :] for c in range(comps) for s in range(pencils)],
        axis=0,
    )
    fwd[...] = split_dot(split_dot(diag_t[...], sides, NT), diag_x[...])

    def solve_step(block, carry):
        base = pl.multiple_of(block * 8, 8)
        first = y_first[pl.ds(base, 8), :]
        last = y_last[pl.ds(base, 8), :]
        weight = y_weight[pl.ds(base, 8), :]
        side_b = fwd[pl.ds(extent + base, 8), :]
        side_c = fwd[pl.ds(2 * extent + base, 8), :]
        out_b, out_c = [], []
        for i in range(8):
            row = slice(i, i + 1)
            row_first = jnp.broadcast_to(first[row], (8, width))
            row_last = jnp.broadcast_to(last[row], (8, width))
            row_weight = jnp.broadcast_to(weight[row], (8, width))
            row_b = jnp.broadcast_to(side_b[row], (8, width))
            row_c = jnp.broadcast_to(side_c[row], (8, width))
            sum_b = sum_c = jnp.zeros((8, width), F32)
            for k in range(0, extent, 8):
                here = slice(k, k + 8)
                there = slice(3 * extent + k, 3 * extent + k + 8)
                z_one, z_two = z_first[here, :], z_last[here, :]
                spectral = (
                    row_first * fwd[here, :]
                    + row_last * fwd[there, :]
                    + row_b * z_one
                    + row_c * z_two
                )
                weights = xz_weight[here, :] + row_weight
                guess = pl.reciprocal(weights, approx=True)
                scaled = spectral * (guess * (2.0 - weights * guess))
                bwd[here, :] += row_first * scaled
                bwd[there, :] += row_last * scaled
                sum_b = sum_b + z_one * scaled
                sum_c = sum_c + z_two * scaled
            out_b.append(sum_b)
            out_c.append(sum_c)
        for start, parts in ((extent, out_b), (2 * extent, out_c)):
            bwd[pl.ds(start + base, 8), :] = jnp.concatenate(
                [jnp.sum(part, axis=0, keepdims=True) for part in parts], axis=0
            )
        return carry

    lax.fori_loop(0, extent // 8, solve_step, 0)
    cells_out = split_dot(diag_x[...], split_dot(diag[...], bwd[...]), NT)
    for s in range(pencils):
        out_send[s] = jnp.concatenate(
            [
                cells_out[c * extent + s * slab : c * extent + (s + 1) * slab, :]
                for c in range(comps)
            ],
            axis=0,
        )
    copies_c = send_pencil(lambda peer: out_send.at[peer], out_in, c_send, c_recv)
    out_in[pencil] = out_send[pencil]
    finish(copies_i)
    all_rows = jnp.concatenate([info_in[h, 0:1, :] for h in range(groups)], axis=1)
    all_ids = jnp.concatenate([info_in[h, 1:2, :] for h in range(groups)], axis=1)
    owner = jnp.concatenate([jnp.full((1, count), h, F32) for h in range(groups)], axis=1)
    share = share_rows * LANES
    local = all_rows - (group * share).astype(F32)
    mine = jnp.logical_and(local >= 0.0, local < share)
    line = jnp.floor(local * (1.0 / LANES))
    met_high = jnp.where(mine, owner * share_rows + line, -1.0)
    met_low = local - line * LANES

    def numbered(size):
        return iota((size, groups * count), 0).astype(F32)

    met_hot = jnp.where(numbered(LANES) == met_low, 1.0, 0.0).astype(BF16)
    met_values = fast_dot(inverse_acc[...].astype(BF16), met_hot)
    met_here = numbered(row_blocks) == met_high
    met_row = jnp.sum(
        jnp.where(met_here, met_values[0:row_blocks], 0.0), axis=0, keepdims=True
    )
    met_lane = jnp.sum(
        jnp.where(met_here, met_values[row_blocks : 2 * row_blocks], 0.0), axis=0, keepdims=True
    )
    meet_rows[...] = jnp.where(
        numbered(mult_rows) == jnp.abs(met_row) - 1.0, jnp.where(met_row > 0.0, 1.0, -1.0), 0.0
    )
    meet_lanes[...] = jnp.where(numbered(LANES) == met_lane, 1.0, 0.0)
    coarse_count = inverse_hbm.shape[0]
    hot_meets[...] = jnp.where(numbered(coarse_count) == all_ids, 1.0, 0.0)
    finish(copies_c)

    for p in range(patches):
        total = out_in[p * dup]
        for u in range(1, dup):
            total = total + out_in[p * dup + u]
        top, rest_part = halves(total)
        table[p * chunk : (p + 1) * chunk, :] = top
        table[table_rows + p * chunk : table_rows + (p + 1) * chunk, :] = rest_part
    lookup = table[...].astype(BF16)
    places = iota((table_rows, LANES), 0).astype(F32)

    def pick_step(offset, carry):
        h = group_peer(offset)
        rows, columns = row_of[h], slot_of[h]
        found = []
        for i in range(0, share_rows, 2):
            hot = jnp.concatenate(
                [
                    one_hot(slot_numbers, columns[i : i + 1]),
                    one_hot(slot_numbers, columns[i + 1 : i + 2]),
                ],
                axis=1,
            )
            both = fast_dot(lookup, hot)
            both = both[0:table_rows] + both[table_rows : 2 * table_rows]
            for u in range(2):
                here = places == rows[i + u : i + u + 1]
                found.append(
                    jnp.sum(
                        jnp.where(here, both[:, u * LANES : (u + 1) * LANES], 0.0),
                        axis=0,
                        keepdims=True,
                    )
                )
        picked[h] = jnp.concatenate(found, axis=0)

        @pl.when(offset < groups)
        def _():
            group_copy(picked.at[h], owner_in, e_send, e_recv, offset, h).start()

        return carry

    lax.fori_loop(1, groups + 1, pick_step, 0)

    owner_in[group] = picked[group]
    prim_high = lax.shift_right_logical(primal, 7)
    prim_low = jnp.bitwise_and(primal, LANES - 1)
    hot_high = jnp.where(iota((row_blocks, count), 0) == prim_high, 1.0, 0.0)
    hot_low = jnp.where(iota((LANES, count), 0) == prim_low, 1.0, 0.0)
    hot_coarse = jnp.where(iota((coarse_count, count), 0) == coarse_ids, 1.0, 0.0)
    flat = jnp.concatenate([picked[h] for h in range(groups)], axis=0)
    primal_values = jnp.sum(hot_dot(flat, hot_low) * hot_high, axis=0, keepdims=True)
    coarse_send[...] = hot_dot(jnp.broadcast_to(primal_values, (8, count)), hot_coarse, NT)[0:1]
    send_all(coarse_send, coarse_in, d_send, d_recv)
    finish(
        [
            group_copy(
                picked.at[group_peer(offset)], owner_in, e_send, e_recv, offset, group_peer(offset)
            )
            for offset in range(1, groups)
        ]
    )

    owners = jnp.concatenate([owner_in[h] for h in range(groups)], axis=0)
    top, rest_part = halves(owners)
    owner_table = jnp.concatenate([top, rest_part], axis=1).astype(BF16)

    def image_step(block, carry):
        base = pl.multiple_of(block * 8, 8)
        lane_base = pl.multiple_of(block * 8 * LANES, 8 * LANES)
        pairs = pair_ref[:, pl.ds(lane_base, 8 * LANES)]
        high = lax.shift_right_logical(pairs, 7)
        low = jnp.bitwise_and(pairs, LANES - 1).astype(F32)
        found = []
        for i in range(8):
            lanes = slice(i * LANES, (i + 1) * LANES)
            hot = jnp.concatenate(
                [one_hot(lane_numbers, low[0:1, lanes]), one_hot(lane_numbers, low[1:2, lanes])],
                axis=1,
            )
            both = fast_dot(owner_table, jnp.concatenate([hot, hot], axis=0))
            place = iota((row_blocks, LANES), 0)
            jump = jnp.where(place == high[0:1, lanes], both[:, 0:LANES], 0.0) - jnp.where(
                place == high[1:2, lanes], both[:, LANES : 2 * LANES], 0.0
            )
            found.append(jnp.sum(jump, axis=0, keepdims=True))
        image[pl.ds(base, 8), :] = jnp.concatenate(found, axis=0)
        return carry

    lax.fori_loop(0, mult_rows // 8, image_step, 0)

    inputs["inverse"].wait()
    finish_all(coarse_send, coarse_in, d_send, d_recv)
    coarse = jnp.sum(coarse_in[...], axis=0)
    lifted = split_dot(jnp.broadcast_to(coarse, (8, coarse_count)), inverse_ref[...], NT)
    lifts = hot_dot(lifted, hot_meets[...])[0:1]
    jump_lift = hot_dot(meet_rows[...] * lifts, meet_lanes[...], NT)

    for name in ("resid", "scale"):
        inputs[name].wait()
    resid, search, scale, jumps = resid_ref[...], dir_ref[...], scale_ref[...], image[...] + jump_lift
    scaled_resid, scaled_jump = scale * resid, scale * jumps

    def total_of(values):
        return jnp.sum(jnp.sum(values, axis=0, keepdims=True), axis=1, keepdims=True)

    parts = [
        total_of(resid * scaled_resid),
        total_of(search * jumps),
        total_of(scaled_resid * jumps),
        total_of(scaled_jump * jumps),
    ]
    lane = iota((1, LANES), 1)
    sums_send[...] = sum(jnp.where(lane == n, value, 0.0) for n, value in enumerate(parts))
    send_all(sums_send, sums_in, f_send, f_recv)
    finish_all(sums_send, sums_in, f_send, f_recv)
    sums = jnp.sum(sums_in[...], axis=0)
    totals = [sums[:, n : n + 1] for n in range(4)]
    old, curvature = totals[0], totals[1]
    alpha = old / curvature
    new = old - 2.0 * alpha * totals[2] + alpha * (alpha * totals[3])
    image_out[...] = jumps
    alpha_out[...] = jnp.broadcast_to(alpha, alpha_out.shape)
    beta_out[...] = jnp.broadcast_to(new / old, beta_out.shape)


def body(
    groups,
    pencils,
    mult_iterate,
    residual,
    direction,
    mult_scale,
    eigen_basis,
    eigen_values,
    elastic_coef,
    coarse_inverse,
    send_pos,
    pair_slots,
    prim_rows,
    coarse_idx,
):
    mult_rows = direction.shape[-1] // LANES
    rows_count = send_pos.shape[-1]
    row_blocks = rows_count // LANES
    share_rows = row_blocks // groups
    patches, _, extent, _ = eigen_basis.shape
    comps = elastic_coef.shape[1]
    pairs = pair_slots.reshape(pair_slots.shape[2:])
    primal, coarse_ids = prim_rows.reshape(1, -1), coarse_idx.reshape(1, -1)
    slab = extent // pencils
    slots = 4 * extent
    width = comps * extent // (pencils // patches)
    chunk = slab * comps
    table_rows = patches * chunk
    coarse_count = coarse_inverse.shape[0]
    primal_count = primal.shape[1]
    devices = groups * pencils

    def vmem(*shape):
        return pltpu.VMEM(shape, F32)

    def index(*shape):
        return pltpu.VMEM(shape, jnp.int32)

    shape = (mult_rows, LANES)
    share = (groups, share_rows, LANES)
    pencil_sems = pltpu.SemaphoreType.DMA((pencils,))
    device_sems = pltpu.SemaphoreType.DMA((devices,))
    group_sems = pltpu.SemaphoreType.DMA((groups,))
    scratch = [
        vmem(2 * row_blocks, LANES),
        vmem(*share),
        vmem(*share),
        vmem(*share),
        vmem(*share),
        vmem(2 * table_rows, slots),
        vmem(patches, chunk, slots),
        vmem(pencils, chunk, slots),
        vmem(slots, slots),
        vmem(slots, slots),
        vmem(comps * extent, width),
        vmem(slots, width),
        vmem(extent, width),
        vmem(extent, width),
        vmem(extent, width),
        vmem(slots, width),
        vmem(pencils, chunk, slots),
        vmem(pencils, chunk, slots),
        vmem(2 * table_rows, slots),
        vmem(*share),
        vmem(1, coarse_count),
        vmem(devices, 1, coarse_count),
        vmem(*share),
        vmem(mult_rows, LANES),
        vmem(1, LANES),
        vmem(devices, 1, LANES),
        vmem(8, primal_count),
        vmem(groups, 8, primal_count),
        vmem(2 * row_blocks, LANES),
        vmem(coarse_count, groups * primal_count),
        vmem(mult_rows, groups * primal_count),
        vmem(LANES, groups * primal_count),
        group_sems,
        group_sems,
        pencil_sems,
        pencil_sems,
        pencil_sems,
        pencil_sems,
        device_sems,
        device_sems,
        group_sems,
        group_sems,
        group_sems,
        group_sems,
        device_sems,
        device_sems,
        vmem(*shape),
        vmem(*shape),
        vmem(*shape),
        vmem(*eigen_basis.shape[1:]),
        vmem(3, patches, extent),
        vmem(comps, patches, 3),
        vmem(coarse_count, coarse_count),
        index(*share),
        index(*pairs.shape),
        index(*primal.shape),
        index(*coarse_ids.shape),
        vmem(extent, width),
        vmem(extent, width),
        vmem(extent, width),
        pltpu.SemaphoreType.DMA((11,)),
    ]
    image, alpha, beta = pl.pallas_call(
        functools.partial(kernel, groups, pencils),
        out_shape=[jax.ShapeDtypeStruct(shape, F32)] * 3,
        in_specs=[pl.BlockSpec(memory_space=pltpu.HBM)] * 11,
        out_specs=[pl.BlockSpec(memory_space=pltpu.VMEM)] * 3,
        scratch_shapes=scratch,
        compiler_params=pltpu.CompilerParams(
            collective_id=0, has_side_effects=True, vmem_limit_bytes=64 * 1024 * 1024 - 65536
        ),
        name="tearing_step",
    )(
        residual.reshape(shape),
        direction.reshape(shape),
        mult_scale.reshape(shape),
        eigen_basis,
        eigen_values.transpose(1, 0, 2),
        elastic_coef.transpose(1, 0, 2),
        coarse_inverse,
        send_pos.reshape(share),
        pairs,
        primal,
        coarse_ids,
    )
    full = mult_iterate.shape
    image, alpha, beta = image.reshape(full), alpha.reshape(full), beta.reshape(full)
    next_resid = residual - alpha * image
    next_dir = mult_scale * next_resid + beta * direction
    return mult_iterate + alpha * direction, next_resid, next_dir


def solution(mesh):
    rows = P("group", "pencil", None)
    in_specs = (
        rows,
        rows,
        rows,
        rows,
        P("group", None, None, None),
        P("group", None, None),
        P("group", None, None),
        P(),
        rows,
        P("group", "pencil", None, None),
        rows,
        rows,
    )
    return jax.shard_map(
        functools.partial(body, mesh.shape["group"], mesh.shape["pencil"]),
        mesh=mesh,
        in_specs=in_specs,
        out_specs=(rows, rows, rows),
        check_vma=False,
    )
```
